32 devices in a mesh: gx: 2 (over x), gy: 4 (over y, core), gz: 4 (over z).
Axes of the slice: x: 2, y: 2, z: 4, core: 2. Of those that a mesh axis runs over, the one named last changes fastest.
Arguments:
- tangent: bfloat16 [32, 8, 32, 512], P(None, 'gx', 'gy', 'gz'), may hold values from -130 to 130
- slopes: bfloat16 [32, 8, 32, 512], P(None, 'gx', 'gy', 'gz'), may hold values from -0.099609375 to 1.09375
- first_kernel: bfloat16 [27, 32, 32], replicated, may hold values from -0.21875 to 0.21875
- second_kernel: bfloat16 [27, 32, 32], replicated, may hold values from -0.21875 to 0.21875
Outputs:
- next_vector: float32 [32, 8, 32, 512], P(None, 'gx', 'gy', 'gz')
- jvp_norm: float32 [1], replicated
The draws below stay inside these ranges and needn't reach their ends.
All inputs are finite; a program needn't handle non-finite values.
Results may differ from the reference program's by a relative error of at most 0.0038.
Values may be sent and summed in bfloat16 or wider, within the bound.
A program may use at most 192 MiB of HBM per device.

```python
import math
import jax
import jax.numpy as jnp

CH = 32
TAPS = 27
NX = 8
NY = 32
NZ = 512


def draw_tangent(key, part):
    key_chan, key_base = jax.random.split(key, 2)
    shape = (CH, NX, NY, NZ)
    chan = jnp.exp(jax.random.uniform(key_chan, (CH, 1, 1, 1), jnp.float32) * math.log(10.0))
    depth = jnp.arange(NX, dtype=jnp.float32).reshape(1, NX, 1, 1) / max(NX - 1, 1)
    base = jnp.clip(jax.random.normal(key_base, shape, jnp.float32), -6.0, 6.0)
    ramp = jnp.exp(math.log(3.0) * depth)
    values = base * chan * ramp * 0.2
    return jnp.clip(values, -130.0, 130.0).astype(jnp.bfloat16)


def block_scale(key, extent, cuts, low, top_value):
    def one(position, shards_of):
        draws = jax.random.uniform(jax.random.fold_in(jax.random.fold_in(key, 6), position), (shards_of,), jnp.float32, low / len(cuts), top_value / len(cuts))
        return jnp.repeat(jnp.exp(draws), extent[position] // shards_of).reshape((-1,) + (1,) * (len(extent) - position - 1))

    gain = one(*cuts[0])
    for cut in cuts[1:]:
        gain = gain * one(*cut)
    return gain


def normal_values(own_key, dims, deviation, most, kind=jnp.bfloat16):
    return jnp.clip(deviation * jax.random.normal(own_key, dims, jnp.float32), -most, most).astype(kind)


def setup_inputs(seed: int = 0) -> dict:
    keys = jax.random.split(jax.random.key(seed), 5)
    return {
        "tangent": draw_tangent(jax.random.fold_in(keys[4], 71), 0),
        "slopes": jnp.clip(-0.099609375 + 1.1933594 * jax.random.uniform(keys[1], (CH, NX, NY, NZ), jnp.float32) ** block_scale(keys[1], (CH, NX, NY, NZ), ((1, 2), (2, 4), (3, 4)), -0.2, 0.2), -0.099609375, 1.09375).astype(jnp.bfloat16),
        "first_kernel": normal_values(keys[2], (TAPS, CH, CH), (TAPS * CH) ** -0.5, 0.21875),
        "second_kernel": normal_values(keys[3], (TAPS, CH, CH), (TAPS * CH) ** -0.5, 0.21875),
    }


def convolve(field, kernel, adjoint):
    size_x, size_y, size_z = (field.shape[1], field.shape[2], field.shape[3])
    padded = jnp.pad(field, ((0, 0), (1, 1), (1, 1), (1, 1)))
    total = jnp.zeros((kernel.shape[1], size_x * size_y * size_z), jnp.float32)
    for a in (-1, 0, 1):
        for b in (-1, 0, 1):
            for c in (-1, 0, 1):
                tap = 9 * (a + 1) + 3 * (b + 1) + (c + 1)
                if adjoint:
                    sa, sb, sc = (1 - a, 1 - b, 1 - c)
                    matrix = kernel[tap].T
                else:
                    sa, sb, sc = (1 + a, 1 + b, 1 + c)
                    matrix = kernel[tap]
                piece = padded[:, sa:sa + size_x, sb:sb + size_y, sc:sc + size_z]
                total = total + jnp.dot(matrix, piece.reshape(piece.shape[0], -1), preferred_element_type=jnp.float32)
    return total.reshape(kernel.shape[1], size_x, size_y, size_z)

def reference(tangent, slopes, first_kernel, second_kernel):
    inner = convolve(tangent, first_kernel, False)
    hidden = (slopes.astype(jnp.float32) * inner).astype(jnp.bfloat16)
    image = convolve(hidden, second_kernel, False)
    image_low = image.astype(jnp.bfloat16)
    jvp_norm = jnp.sqrt(jnp.sum(image * image) + 1e-06)
    back = convolve(image_low, second_kernel, True)
    pulled = (slopes.astype(jnp.float32) * back).astype(jnp.bfloat16)
    next_vector = convolve(pulled, first_kernel, True) / jvp_norm
    return (next_vector, jvp_norm.reshape(1))
```

```python
import functools
import itertools

import jax
import jax.numpy as jnp
from jax import lax
from jax.experimental import pallas as pl
from jax.experimental.pallas import tpu as pltpu
from jax.sharding import PartitionSpec as P

AXES = ("gx", "gy", "gz")
MESH = pl.DeviceIdType.MESH
PAD = 16
DIRS = [d for d in itertools.product((-1, 0, 1), repeat=3) if d != (0, 0, 0)]


def kernel(
    counts, ch, t_ref, s_ref, k1t_ref, k2t_ref, k2_ref, k1_ref, out_ref, norm_ref,
    field, edge, rows, shifted, taps, weights, sums_x, sums_y, sums_z,
    send_sem, recv_sem, sum_send, sum_recv,
):
    nx, nz, lanes = t_ref.shape
    ny = lanes // ch
    wide = field.shape[3]
    me = tuple(lax.axis_index(a) for a in AXES)

    def inside(d, sign):
        ok = jnp.bool_(True)
        for m, n, s in zip(me, counts, d):
            if s * sign > 0:
                ok = jnp.logical_and(ok, m < n - 1)
            elif s * sign < 0:
                ok = jnp.logical_and(ok, m > 0)
        return ok

    def others(axis):
        n = counts[axis]
        for k in range(1, n):
            there = list(me)
            there[axis] = lax.rem(me[axis] + k, n)
            yield k, tuple(there)

    field[...] = jnp.zeros_like(field)
    rows[...] = jnp.zeros_like(rows)

    barrier = pltpu.get_barrier_semaphore()
    total = jnp.int32(0)
    for d in DIRS:
        ok = inside(d, 1)
        total = total + ok.astype(jnp.int32)

        @pl.when(ok)
        def _():
            there = tuple(m + s for m, s in zip(me, d))
            pl.semaphore_signal(barrier, inc=1, device_id=there, device_id_type=MESH)

    for axis in range(3):
        for _, there in others(axis):
            pl.semaphore_signal(barrier, inc=1, device_id=there, device_id_type=MESH)
            total = total + 1

    def copy_of(r, i):
        dx, dy, dz = DIRS[i]
        if dz == 0:
            z_from, z_to, size = PAD, PAD, nz
        elif dz > 0:
            z_from, z_to, size = nz, 0, PAD
        else:
            z_from, z_to, size = PAD, nz + PAD, PAD
        if dy == 0:
            if dx == 0:
                x_from, x_to, planes = 1, 1, nx
            elif dx > 0:
                x_from, x_to, planes = nx, 0, 1
            else:
                x_from, x_to, planes = 1, nx + 1, 1
            src = field.at[r, pl.ds(x_from, planes), pl.ds(z_from, size), pl.ds(0, lanes)]
            dst = field.at[r, pl.ds(x_to, planes), pl.ds(z_to, size), pl.ds(0, lanes)]
        else:
            src = edge.at[r, (dy + 1) // 2, pl.ds(z_from - PAD, size), :]
            dst = rows.at[r, dx + 1, (1 - dy) // 2, pl.ds(z_to, size), :]
        there = tuple(
            m if s == 0 else jnp.clip(m + s, 0, n - 1) for m, s, n in zip(me, DIRS[i], counts)
        )
        return pltpu.make_async_remote_copy(
            src_ref=src, dst_ref=dst, send_sem=send_sem.at[r, i], recv_sem=recv_sem.at[r, i],
            device_id=there, device_id_type=MESH,
        )

    def sum_copies(axis, buf):
        return [
            pltpu.make_async_remote_copy(
                src_ref=buf.at[me[axis]], dst_ref=buf.at[me[axis]],
                send_sem=sum_send.at[axis, k], recv_sem=sum_recv.at[axis, k],
                device_id=there, device_id_type=MESH,
            )
            for k, there in others(axis)
        ]

    def start_sum(axis, buf, value):
        buf[me[axis]] = value
        for copy in sum_copies(axis, buf):
            copy.start()

    def finish_sum(axis, buf):
        for copy in sum_copies(axis, buf):
            copy.wait()
        result = buf[0]
        for j in range(1, counts[axis]):
            result = result + buf[j]
        return result

    lane_block = lax.broadcasted_iota(jnp.int32, (ch, lanes), 1) // ch
    lane_inner = lax.rem(lax.broadcasted_iota(jnp.int32, (ch, lanes), 1), ch)
    tiler = (lax.broadcasted_iota(jnp.int32, (ch, lanes), 0) == lane_inner)
    tiler = tiler.astype(jnp.float32).astype(jnp.bfloat16)

    def build(k_ref, flip):
        taps[...] = jnp.dot(k_ref[...], tiler, preferred_element_type=jnp.float32)

        def group(g, carry):
            mats = []
            for b in range(3):
                tap = 9 * (g // 3) + 3 * b + g % 3
                tap = 26 - tap if flip else tap
                mats.append(taps[pl.ds(pl.multiple_of(tap * ch, ch), ch), :])
            strips = []
            for y in list(range(ny)) + [-1, ny]:
                strip = jnp.zeros((ch, lanes), jnp.float32)
                for b in range(3):
                    if 0 <= y - (b - 1) < ny:
                        strip = jnp.where(lane_block == y - (b - 1), mats[b], strip)
                strips.append(strip)
            strips.append(jnp.zeros((wide - (ny + 2) * ch, lanes), jnp.float32))
            tile = jnp.concatenate(strips, axis=0).astype(jnp.bfloat16)
            weights[pl.ds(pl.multiple_of(g * wide, wide), wide), :] = tile
            return carry

        lax.fori_loop(0, 9, group, 0)

    def conv(r, value, k_ref, flip):
        value = value.reshape(nx, nz, lanes)
        field[r, 1 : nx + 1, PAD : PAD + nz, 0:lanes] = value
        for s in range(2):
            low = s * (ny - 1) * ch
            for x in range(nx):
                edge[r, s, :, x * ch : (x + 1) * ch] = value[x, :, low : low + ch]
        if r == 0:
            pl.semaphore_wait(barrier, total)
        for i, d in enumerate(DIRS):
            @pl.when(inside(d, 1))
            def _():
                copy_of(r, i).start()
        build(k_ref, flip)
        for i, d in enumerate(DIRS):
            @pl.when(inside(d, -1))
            def _():
                copy_of(r, i).wait_recv()
        for s in range(2):
            low = lanes + s * ch
            field[r, 0, :, low : low + ch] = rows[r, 2, s, :, (nx - 1) * ch : nx * ch]
            for x in range(nx):
                field[r, 1 + x, :, low : low + ch] = rows[r, 1, s, :, x * ch : (x + 1) * ch]
            field[r, nx + 1, :, low : low + ch] = rows[r, 0, s, :, 0:ch]
        for c in range(3):
            shifted[c] = field[r, :, PAD - 1 + c : PAD - 1 + c + nz, :]
        pieces = [
            shifted[c, a : a + nx].reshape(nx * nz, wide) for a in range(3) for c in range(3)
        ]
        stacked = jnp.concatenate(pieces, axis=1)
        return jnp.dot(stacked, weights[...], preferred_element_type=jnp.float32)

    slopes = s_ref[...].reshape(nx * nz, lanes).astype(jnp.float32)
    inner = conv(0, t_ref[...], k1t_ref, False)
    hidden = (slopes * inner).astype(jnp.bfloat16)
    image = conv(1, hidden, k2t_ref, False)
    squares = image * image
    squares = squares[:, 0:128] + squares[:, 128:256]
    start_sum(0, sums_x, jnp.sum(squares.reshape(nx * nz // 8, 8, 128), axis=0))
    back = conv(2, image.astype(jnp.bfloat16), k2_ref, True)
    start_sum(1, sums_y, finish_sum(0, sums_x))
    slopes = s_ref[...].reshape(nx * nz, lanes).astype(jnp.float32)
    pulled = (slopes * back).astype(jnp.bfloat16)
    result = conv(3, pulled, k1_ref, True)
    start_sum(2, sums_z, finish_sum(1, sums_y))
    out_ref[...] = result.reshape(nx, nz, lanes)
    norm = jnp.sqrt(jnp.sum(finish_sum(2, sums_z), keepdims=True) + 1e-06)
    norm_ref[...] = norm
    out_ref[...] = out_ref[...] / norm.reshape(1, 1, 1)

    for r in range(4):
        for i, d in enumerate(DIRS):
            @pl.when(inside(d, 1))
            def _():
                copy_of(r, i).wait_send()


def on_device(counts, tangent, slopes, first_kernel, second_kernel):
    ch, nx, ny, nz = tangent.shape
    lanes = ny * ch
    wide = lanes + 128

    def spread(array):
        return jnp.transpose(array, (1, 3, 2, 0)).reshape(nx, nz, lanes)

    def flat(array):
        return array.reshape(-1, ch)

    first_t = jnp.swapaxes(first_kernel, 1, 2)
    second_t = jnp.swapaxes(second_kernel, 1, 2)
    most = max(counts)
    result, norm = pl.pallas_call(
        functools.partial(kernel, counts, ch),
        out_shape=(
            jax.ShapeDtypeStruct((nx, nz, lanes), jnp.float32),
            jax.ShapeDtypeStruct((1, 1), jnp.float32),
        ),
        in_specs=[pl.BlockSpec(memory_space=pltpu.VMEM)] * 6,
        out_specs=(pl.BlockSpec(memory_space=pltpu.VMEM),) * 2,
        scratch_shapes=[
            pltpu.VMEM((4, nx + 2, nz + 2 * PAD, wide), jnp.bfloat16),
            pltpu.VMEM((4, 2, nz, nx * ch), jnp.bfloat16),
            pltpu.VMEM((4, 3, 2, nz + 2 * PAD, nx * ch), jnp.bfloat16),
            pltpu.VMEM((3, nx + 2, nz, wide), jnp.bfloat16),
            pltpu.VMEM((27 * ch, lanes), jnp.float32),
            pltpu.VMEM((9 * wide, lanes), jnp.bfloat16),
            pltpu.VMEM((counts[0], 8, 128), jnp.float32),
            pltpu.VMEM((counts[1], 8, 128), jnp.float32),
            pltpu.VMEM((counts[2], 8, 128), jnp.float32),
            pltpu.SemaphoreType.DMA((4, len(DIRS))),
            pltpu.SemaphoreType.DMA((4, len(DIRS))),
            pltpu.SemaphoreType.DMA((3, most)),
            pltpu.SemaphoreType.DMA((3, most)),
        ],
        compiler_params=pltpu.CompilerParams(
            collective_id=0, has_side_effects=True, vmem_limit_bytes=48 * 1024 * 1024
        ),
        name="denoiser_step",
    )(spread(tangent), spread(slopes), flat(first_t), flat(second_t), flat(second_kernel), flat(first_kernel))
    result = result.reshape(nx, nz, ny, ch)
    return (jnp.transpose(result, (3, 0, 2, 1)), norm.reshape(1))


def solution(mesh):
    counts = tuple(mesh.shape[a] for a in AXES)
    return jax.shard_map(
        functools.partial(on_device, counts),
        mesh=mesh,
        in_specs=(P(None, "gx", "gy", "gz"), P(None, "gx", "gy", "gz"), P(), P()),
        out_specs=(P(None, "gx", "gy", "gz"), P()),
        check_vma=False,
    )
```

```python
import functools
import itertools

import jax
import jax.numpy as jnp
from jax import lax
from jax.experimental import pallas as pl
from jax.experimental.pallas import tpu as pltpu
from jax.sharding import PartitionSpec as P

AXES = ("gx", "gy", "gz")
MESH = pl.DeviceIdType.MESH
PAD = 16
DIRS = sorted(
    (d for d in itertools.product((-1, 0, 1), repeat=3) if d != (0, 0, 0)),
    key=lambda d: (d[1:] != (0, 0), sum(map(abs, d)), abs(d[0])),
)


def kernel(
    counts, ch, t_ref, s_ref, k1t_ref, k2t_ref, k2_ref, k1_ref, out_ref, norm_ref,
    field, edge, edge_x, rows, rows_x, shifted, shifted_x, acc, taps, weights, sums_x, sums_y, sums_z,
    send_sem, recv_sem, sum_send, sum_recv,
):
    nx, nz, lanes = t_ref.shape
    ny = lanes // ch
    wide = field.shape[3]
    me = tuple(lax.axis_index(a) for a in AXES)

    def inside(d, sign):
        ok = jnp.bool_(True)
        for m, n, s in zip(me, counts, d):
            if s * sign > 0:
                ok = jnp.logical_and(ok, m < n - 1)
            elif s * sign < 0:
                ok = jnp.logical_and(ok, m > 0)
        return ok

    def others(axis):
        n = counts[axis]
        for k in range(1, n):
            there = list(me)
            there[axis] = lax.rem(me[axis] + k, n)
            yield k, tuple(there)

    field[...] = jnp.zeros_like(field)
    rows[...] = jnp.zeros_like(rows)
    rows_x[...] = jnp.zeros_like(rows_x)
    shifted[...] = jnp.zeros_like(shifted)

    barrier = pltpu.get_barrier_semaphore()
    total = jnp.int32(0)
    for d in DIRS:
        ok = inside(d, 1)
        total = total + ok.astype(jnp.int32)

        @pl.when(ok)
        def _():
            there = tuple(m + s for m, s in zip(me, d))
            pl.semaphore_signal(barrier, inc=1, device_id=there, device_id_type=MESH)

    for axis in range(3):
        for _, there in others(axis):
            pl.semaphore_signal(barrier, inc=1, device_id=there, device_id_type=MESH)
            total = total + 1

    def copy_of(r, i):
        dx, dy, dz = DIRS[i]
        if dz == 0:
            z_from, z_to, size = PAD, PAD, nz
        elif dz > 0:
            z_from, z_to, size = nz, 0, PAD
        else:
            z_from, z_to, size = PAD, nz + PAD, PAD
        if dy == 0:
            if dx == 0:
                x_from, x_to, planes = 1, 1, nx
            elif dx > 0:
                x_from, x_to, planes = nx, 0, 1
            else:
                x_from, x_to, planes = 1, nx + 1, 1
            src = field.at[r, pl.ds(x_from, planes), pl.ds(z_from, size), pl.ds(0, lanes)]
            dst = field.at[r, pl.ds(x_to, planes), pl.ds(z_to, size), pl.ds(0, lanes)]
        elif dx != 0 and dz == 0:
            src = edge_x.at[r, (dx + 1) // 2, (dy + 1) // 2]
            dst = rows_x.at[r, (dx + 1) // 2, (1 - dy) // 2]
        else:
            src = edge.at[r, (dy + 1) // 2, pl.ds(z_from - PAD, size), :]
            dst = rows.at[r, dx + 1, (1 - dy) // 2, pl.ds(z_to, size), :]
        there = tuple(
            m if s == 0 else jnp.clip(m + s, 0, n - 1) for m, s, n in zip(me, DIRS[i], counts)
        )
        return pltpu.make_async_remote_copy(
            src_ref=src, dst_ref=dst, send_sem=send_sem.at[r, i], recv_sem=recv_sem.at[r, i],
            device_id=there, device_id_type=MESH,
        )

    def sum_copies(axis, buf):
        return [
            pltpu.make_async_remote_copy(
                src_ref=buf.at[me[axis]], dst_ref=buf.at[me[axis]],
                send_sem=sum_send.at[axis, k], recv_sem=sum_recv.at[axis, k],
                device_id=there, device_id_type=MESH,
            )
            for k, there in others(axis)
        ]

    def start_sum(axis, buf, value):
        buf[me[axis]] = value
        for copy in sum_copies(axis, buf):
            copy.start()

    def finish_sum(axis, buf):
        for copy in sum_copies(axis, buf):
            copy.wait()
        result = buf[0]
        for j in range(1, counts[axis]):
            result = result + buf[j]
        return result

    lane_block = lax.broadcasted_iota(jnp.int32, (ch, lanes), 1) // ch
    lane_inner = lax.rem(lax.broadcasted_iota(jnp.int32, (ch, lanes), 1), ch)
    tiler = (lax.broadcasted_iota(jnp.int32, (ch, lanes), 0) == lane_inner)
    tiler = tiler.astype(jnp.float32).astype(jnp.bfloat16)

    def build(k_ref, flip):
        taps[...] = jnp.dot(k_ref[...], tiler, preferred_element_type=jnp.float32)

        def group(g, carry):
            mats = []
            for b in range(3):
                tap = 9 * (g // 3) + 3 * b + g % 3
                tap = 26 - tap if flip else tap
                mats.append(taps[pl.ds(pl.multiple_of(tap * ch, ch), ch), :])
            strips = []
            for y in list(range(ny)) + [-1, ny]:
                strip = jnp.zeros((ch, lanes), jnp.float32)
                for b in range(3):
                    if 0 <= y - (b - 1) < ny:
                        strip = jnp.where(lane_block == y - (b - 1), mats[b], strip)
                strips.append(strip)
            strips.append(jnp.zeros((wide - (ny + 2) * ch, lanes), jnp.float32))
            tile = jnp.concatenate(strips, axis=0).astype(jnp.bfloat16)
            weights[pl.ds(pl.multiple_of(g * wide, wide), wide), :] = tile
            return carry

        lax.fori_loop(0, 9, group, 0)

    def conv(r, value, k_ref, flip):
        value = value.reshape(nx, nz, lanes)
        field[r, 1 : nx + 1, PAD : PAD + nz, 0:lanes] = value
        parts = 128 // ch
        quarter = nz // parts
        for s in range(2):
            low = s * (ny - 1) * ch
            for x in range(nx):
                edge[r, s, :, x * ch : (x + 1) * ch] = value[x, :, low : low + ch]
            for side, x in enumerate((0, nx - 1)):
                for q in range(parts):
                    edge_x[r, side, s, :, q * ch : (q + 1) * ch] = value[
                        x, q * quarter : (q + 1) * quarter, low : low + ch
                    ]
        if r == 0:
            pl.semaphore_wait(barrier, total)
        for i, d in enumerate(DIRS):
            @pl.when(inside(d, 1))
            def _():
                copy_of(r, i).start()
        build(k_ref, flip)
        def arrive(along_x):
            for i, d in enumerate(DIRS):
                if (d[0] != 0) == along_x:
                    @pl.when(inside(d, -1))
                    def _():
                        copy_of(r, i).wait_recv()

        arrive(False)
        for s in range(2):
            low = lanes + s * ch
            for x in range(nx):
                field[r, 1 + x, :, low : low + ch] = rows[r, 1, s, :, x * ch : (x + 1) * ch]
        for c in range(3):
            shifted[c, 1 : nx + 1] = field[r, 1 : nx + 1, PAD - 1 + c : PAD - 1 + c + nz, :]
        pieces = [
            shifted[c, a : a + nx].reshape(nx * nz, wide) for a in range(3) for c in range(3)
        ]
        stacked = jnp.concatenate(pieces, axis=1)
        acc[...] = jnp.dot(stacked, weights[...], preferred_element_type=jnp.float32)
        if r == 2:
            start_sum(1, sums_y, finish_sum(0, sums_x))
        arrive(True)
        for side, plane, out, a in ((1, 0, 0, 0), (0, nx + 1, nx - 1, 2)):
            @pl.when(inside((2 * side - 1, 0, 0), -1))
            def _():
                x = nx - 1 if side else 0
                for s in range(2):
                    low = lanes + s * ch
                    for z in (0, nz + PAD):
                        field[r, plane, z : z + PAD, low : low + ch] = rows[
                            r, 2 * side, s, z : z + PAD, x * ch : (x + 1) * ch
                        ]
                    for q in range(parts):
                        z = PAD + q * quarter
                        field[r, plane, z : z + quarter, low : low + ch] = rows_x[
                            r, side, s, :, q * ch : (q + 1) * ch
                        ]
                for c in range(3):
                    shifted_x[c] = field[r, plane, PAD - 1 + c : PAD - 1 + c + nz, :]
                more = jnp.dot(
                    jnp.concatenate([shifted_x[c] for c in range(3)], axis=1),
                    weights[3 * a * wide : 3 * (a + 1) * wide, :],
                    preferred_element_type=jnp.float32,
                )
                acc[out * nz : (out + 1) * nz, :] += more
        return acc[...]

    slopes = s_ref[...].reshape(nx * nz, lanes).astype(jnp.float32)
    inner = conv(0, t_ref[...], k1t_ref, False)
    hidden = (slopes * inner).astype(jnp.bfloat16)
    image = conv(1, hidden, k2t_ref, False)
    squares = image * image
    squares = squares[:, 0:128] + squares[:, 128:256]
    start_sum(0, sums_x, jnp.sum(squares.reshape(nx * nz // 8, 8, 128), axis=0))
    back = conv(2, image.astype(jnp.bfloat16), k2_ref, True)
    start_sum(2, sums_z, finish_sum(1, sums_y))
    slopes = s_ref[...].reshape(nx * nz, lanes).astype(jnp.float32)
    pulled = (slopes * back).astype(jnp.bfloat16)
    result = conv(3, pulled, k1_ref, True)
    norm = jnp.sqrt(jnp.sum(finish_sum(2, sums_z), keepdims=True) + 1e-06)
    norm_ref[...] = norm
    out_ref[...] = (result / norm).reshape(nx, nz, lanes)

    for r in range(4):
        for i, d in enumerate(DIRS):
            @pl.when(inside(d, 1))
            def _():
                copy_of(r, i).wait_send()


def on_device(counts, tangent, slopes, first_kernel, second_kernel):
    ch, nx, ny, nz = tangent.shape
    lanes = ny * ch
    wide = lanes + 128

    def spread(array):
        return jnp.transpose(array, (1, 3, 2, 0)).reshape(nx, nz, lanes)

    def flat(array):
        return array.reshape(-1, ch)

    first_t = jnp.swapaxes(first_kernel, 1, 2)
    second_t = jnp.swapaxes(second_kernel, 1, 2)
    most = max(counts)
    result, norm = pl.pallas_call(
        functools.partial(kernel, counts, ch),
        out_shape=(
            jax.ShapeDtypeStruct((nx, nz, lanes), jnp.float32),
            jax.ShapeDtypeStruct((1, 1), jnp.float32),
        ),
        in_specs=[pl.BlockSpec(memory_space=pltpu.VMEM)] * 6,
        out_specs=(pl.BlockSpec(memory_space=pltpu.VMEM),) * 2,
        scratch_shapes=[
            pltpu.VMEM((4, nx + 2, nz + 2 * PAD, wide), jnp.bfloat16),
            pltpu.VMEM((4, 2, nz, nx * ch), jnp.bfloat16),
            pltpu.VMEM((4, 2, 2, nz * ch // 128, 128), jnp.bfloat16),
            pltpu.VMEM((4, 3, 2, nz + 2 * PAD, nx * ch), jnp.bfloat16),
            pltpu.VMEM((4, 2, 2, nz * ch // 128, 128), jnp.bfloat16),
            pltpu.VMEM((3, nx + 2, nz, wide), jnp.bfloat16),
            pltpu.VMEM((3, nz, wide), jnp.bfloat16),
            pltpu.VMEM((nx * nz, lanes), jnp.float32),
            pltpu.VMEM((27 * ch, lanes), jnp.float32),
            pltpu.VMEM((9 * wide, lanes), jnp.bfloat16),
            pltpu.VMEM((counts[0], 8, 128), jnp.float32),
            pltpu.VMEM((counts[1], 8, 128), jnp.float32),
            pltpu.VMEM((counts[2], 8, 128), jnp.float32),
            pltpu.SemaphoreType.DMA((4, len(DIRS))),
            pltpu.SemaphoreType.DMA((4, len(DIRS))),
            pltpu.SemaphoreType.DMA((3, most)),
            pltpu.SemaphoreType.DMA((3, most)),
        ],
        compiler_params=pltpu.CompilerParams(
            collective_id=0, has_side_effects=True, vmem_limit_bytes=48 * 1024 * 1024
        ),
        name="denoiser_step",
    )(spread(tangent), spread(slopes), flat(first_t), flat(second_t), flat(second_kernel), flat(first_kernel))
    result = result.reshape(nx, nz, ny, ch)
    return (jnp.transpose(result, (3, 0, 2, 1)), norm.reshape(1))


def solution(mesh):
    counts = tuple(mesh.shape[a] for a in AXES)
    return jax.shard_map(
        functools.partial(on_device, counts),
        mesh=mesh,
        in_specs=(P(None, "gx", "gy", "gz"), P(None, "gx", "gy", "gz"), P(), P()),
        out_specs=(P(None, "gx", "gy", "gz"), P()),
        check_vma=False,
    )
```

```python
import functools
import itertools

import jax
import jax.numpy as jnp
from jax import lax
from jax.experimental import pallas as pl
from jax.experimental.pallas import tpu as pltpu
from jax.sharding import PartitionSpec as P

AXES = ("gx", "gy", "gz")
MESH = pl.DeviceIdType.MESH
PAD = 16
DIRS = sorted(
    (d for d in itertools.product((-1, 0, 1), repeat=3) if d != (0, 0, 0)),
    key=lambda d: (d[1:] != (0, 0), sum(map(abs, d)), abs(d[0])),
)


def kernel(
    counts, ch, t_ref, s_ref, k1t_ref, k2t_ref, k2_ref, k1_ref, out_ref, norm_ref,
    field, slopes, edge, edge_x, rows, rows_x, line,
    shifted, shifted_y, shifted_x, acc, taps, weights, sums_x, sums_y, sums_z,
    send_sem, recv_sem, slope_send, slope_recv, sum_send, sum_recv,
):
    nx, nz, lanes = t_ref.shape
    ny = lanes // ch
    ext = nz + 2 * PAD
    own = 2 * PAD
    parts = 128 // ch
    per_a = 4 * lanes
    me = tuple(lax.axis_index(a) for a in AXES)

    def inside(d, sign):
        ok = jnp.bool_(True)
        for m, n, s in zip(me, counts, d):
            if s * sign > 0:
                ok = jnp.logical_and(ok, m < n - 1)
            elif s * sign < 0:
                ok = jnp.logical_and(ok, m > 0)
        return ok

    def others(axis):
        n = counts[axis]
        for k in range(1, n):
            there = list(me)
            there[axis] = lax.rem(me[axis] + k, n)
            yield k, tuple(there)

    for buf in (field, slopes, rows, rows_x, line, shifted, shifted_y, shifted_x, weights):
        buf[...] = jnp.zeros_like(buf)

    barrier = pltpu.get_barrier_semaphore()
    total = jnp.int32(0)
    for d in DIRS:
        ok = inside(d, 1)
        total = total + ok.astype(jnp.int32)

        @pl.when(ok)
        def _():
            there = tuple(m + s for m, s in zip(me, d))
            pl.semaphore_signal(barrier, inc=1, device_id=there, device_id_type=MESH)

    for axis in range(3):
        for _, there in others(axis):
            pl.semaphore_signal(barrier, inc=1, device_id=there, device_id_type=MESH)
            total = total + 1

    def remote(src, dst, send, recv, d):
        there = tuple(
            m if s == 0 else jnp.clip(m + s, 0, n - 1) for m, s, n in zip(me, d, counts)
        )
        return pltpu.make_async_remote_copy(
            src_ref=src, dst_ref=dst, send_sem=send, recv_sem=recv,
            device_id=there, device_id_type=MESH,
        )

    def copy_of(r, i):
        dx, dy, dz = DIRS[i]
        if dz == 0:
            z_from, z_to, size = (own, own, nz) if r == 0 else (PAD, PAD, ext)
        elif dz > 0:
            z_from, z_to, size = own + nz - PAD, PAD, PAD
        else:
            z_from, z_to, size = own, own + nz, PAD
        if dy == 0:
            if dx == 0:
                x_from, x_to, planes = 1, 1, nx
            elif dx > 0:
                x_from, x_to, planes = nx, 0, 1
            else:
                x_from, x_to, planes = 1, nx + 1, 1
            src = field.at[r, pl.ds(x_from, planes), pl.ds(z_from, size), :]
            dst = field.at[r, pl.ds(x_to, planes), pl.ds(z_to, size), :]
        elif dx != 0 and dz == 0:
            size = (nz if r == 0 else nz + 4 * PAD) // parts
            src = edge_x.at[r, (dx + 1) // 2, (dy + 1) // 2, pl.ds(0, size), :]
            dst = rows_x.at[r, (dx + 1) // 2, (1 - dy) // 2, pl.ds(0, size), :]
        else:
            src = edge.at[r, (dy + 1) // 2, pl.ds(z_from, size), :]
            dst = rows.at[r, dx + 1, (1 - dy) // 2, pl.ds(z_to, size), :]
        return remote(src, dst, send_sem.at[r, i], recv_sem.at[r, i], DIRS[i])

    def dirs_of(r):
        return [(i, d) for i, d in enumerate(DIRS) if r == 0 or d[2] == 0]

    def slope_copy(side):
        z_from, z_to = (nz, 0) if side else (PAD, nz + PAD)
        return remote(
            slopes.at[:, pl.ds(z_from, PAD), :], slopes.at[:, pl.ds(z_to, PAD), :],
            slope_send.at[side], slope_recv.at[side], (0, 0, 2 * side - 1),
        )

    def sum_copies(axis, buf):
        return [
            pltpu.make_async_remote_copy(
                src_ref=buf.at[me[axis]], dst_ref=buf.at[me[axis]],
                send_sem=sum_send.at[axis, k], recv_sem=sum_recv.at[axis, k],
                device_id=there, device_id_type=MESH,
            )
            for k, there in others(axis)
        ]

    def start_sum(axis, buf, value):
        buf[me[axis]] = value
        for copy in sum_copies(axis, buf):
            copy.start()

    def finish_sum(axis, buf):
        for copy in sum_copies(axis, buf):
            copy.wait()
        result = buf[0]
        for j in range(1, counts[axis]):
            result = result + buf[j]
        return result

    lane_block = lax.broadcasted_iota(jnp.int32, (ch, lanes), 1) // ch
    lane_inner = lax.rem(lax.broadcasted_iota(jnp.int32, (ch, lanes), 1), ch)
    tiler = (lax.broadcasted_iota(jnp.int32, (ch, lanes), 0) == lane_inner)
    tiler = tiler.astype(jnp.float32).astype(jnp.bfloat16)

    def build(r):
        k_ref, flip = ((k1t_ref, 0), (k2t_ref, 0), (k2_ref, 1), (k1_ref, 1))[r]
        taps[...] = jnp.dot(k_ref[...], tiler, preferred_element_type=jnp.float32)

        def group(g, carry):
            mats = []
            for b in range(3):
                tap = 9 * (g // 3) + 3 * b + g % 3
                tap = 26 - tap if flip else tap
                mats.append(taps[pl.ds(pl.multiple_of(tap * ch, ch), ch), :])
            strips = []
            for y in list(range(ny)) + [-1, ny]:
                strip = jnp.zeros((ch, lanes), jnp.float32)
                for b in range(3):
                    if 0 <= y - (b - 1) < ny:
                        strip = jnp.where(lane_block == y - (b - 1), mats[b], strip)
                strips.append(strip)
            base = per_a * (g // 3)
            at = pl.multiple_of(base + lanes * (g % 3), ch)
            main = jnp.concatenate(strips[:ny], axis=0)
            weights[r % 2, pl.ds(at, lanes), :] = main.astype(jnp.bfloat16)
            at = pl.multiple_of(base + 3 * lanes + 2 * ch * (g % 3), ch)
            outer = jnp.concatenate(strips[ny:], axis=0)
            weights[r % 2, pl.ds(at, 2 * ch), :] = outer.astype(jnp.bfloat16)
            return carry

        lax.fori_loop(0, 9, group, 0)

    def conv(r):
        z, size = (own, nz) if r == 0 else (PAD, ext)
        for s in range(2):
            low = s * (ny - 1) * ch
            for x in range(nx):
                edge[r, s, z : z + size, x * ch : (x + 1) * ch] = field[
                    r, 1 + x, z : z + size, low : low + ch
                ]
        start, piece = (own, nz // parts) if r == 0 else (0, (nz + 4 * PAD) // parts)
        for s in range(2):
            low = s * (ny - 1) * ch
            for side, x in enumerate((0, nx - 1)):
                for q in range(parts):
                    z = start + q * piece
                    edge_x[r, side, s, 0:piece, q * ch : (q + 1) * ch] = field[
                        r, 1 + x, z : z + piece, low : low + ch
                    ]
        if r == 0:
            build(0)
            pl.semaphore_wait(barrier, total)
        for i, d in dirs_of(r):
            @pl.when(inside(d, 1))
            def _():
                copy_of(r, i).start()

        def arrive(keep):
            for i, d in dirs_of(r):
                if keep(d):
                    @pl.when(inside(d, -1))
                    def _():
                        copy_of(r, i).wait_recv()

        if r == 0:
            for side in range(2):
                @pl.when(inside((0, 0, 2 * side - 1), 1))
                def _():
                    slope_copy(side).start()

        arrive(lambda d: d[0] == 0 and d[1] == 0)
        lo, size = (PAD, nz) if r == 3 else (0, ext)
        for c in range(3):
            z = PAD - 1 + c + lo
            shifted[c, 1 : nx + 1, lo : lo + size, :] = field[r, 1 : nx + 1, z : z + size, :]

        def weight_rows(first, count):
            return jnp.concatenate(
                [weights[r % 2, a * per_a + first : a * per_a + first + count, :] for a in range(3)],
                axis=0,
            )

        pieces = [
            shifted[c, a : a + nx, lo : lo + size, :].reshape(nx * size, lanes)
            for a in range(3) for c in range(3)
        ]
        acc[0 : nx * size, :] = jnp.dot(
            jnp.concatenate(pieces, axis=1), weight_rows(0, 3 * lanes),
            preferred_element_type=jnp.float32,
        )
        if r < 3:
            build(r + 1)
        arrive(lambda d: d[0] == 0 and d[1] != 0)
        for c in range(3):
            z = PAD - 1 + c + lo
            for s in range(2):
                low = (2 * c + s) * ch
                for x in range(nx):
                    shifted_y[1 + x, lo : lo + size, low : low + ch] = rows[
                        r, 1, s, z : z + size, x * ch : (x + 1) * ch
                    ]
        pieces = [
            shifted_y[a : a + nx, lo : lo + size, :].reshape(nx * size, lanes) for a in range(3)
        ]
        acc[0 : nx * size, :] += jnp.dot(
            jnp.concatenate(pieces, axis=1), weight_rows(3 * lanes, lanes),
            preferred_element_type=jnp.float32,
        )
        if r == 2:
            start_sum(1, sums_y, finish_sum(0, sums_x))
        arrive(lambda d: d[0] != 0)
        for side, plane, out, a in ((1, 0, 0, 0), (0, nx + 1, nx - 1, 2)):
            @pl.when(inside((2 * side - 1, 0, 0), -1))
            def _():
                x = nx - 1 if side else 0
                for s in range(2):
                    if r == 0:
                        for z in (PAD, own + nz):
                            line[s, z : z + PAD, 0:ch] = rows[
                                r, 2 * side, s, z : z + PAD, x * ch : (x + 1) * ch
                            ]
                    for q in range(parts):
                        z = start + q * piece
                        line[s, z : z + piece, 0:ch] = rows_x[
                            r, side, s, 0:piece, q * ch : (q + 1) * ch
                        ]
                for c in range(3):
                    z = PAD - 1 + c + lo
                    shifted_x[lo : lo + size, c * lanes : (c + 1) * lanes] = field[
                        r, plane, z : z + size, :
                    ]
                    for s in range(2):
                        low = 3 * lanes + (2 * c + s) * ch
                        shifted_x[lo : lo + size, low : low + ch] = line[s, z : z + size, 0:ch]
                acc[out * size : (out + 1) * size, :] += jnp.dot(
                    shifted_x[lo : lo + size, :], weights[r % 2, a * per_a : (a + 1) * per_a, :],
                    preferred_element_type=jnp.float32,
                )
        return acc[0 : nx * size, :].reshape(nx, size, lanes)

    slopes[:, PAD : PAD + nz, :] = s_ref[...]
    field[0, 1 : nx + 1, own : own + nz, :] = t_ref[...]
    inner = conv(0)
    for side in range(2):
        @pl.when(inside((0, 0, 2 * side - 1), -1))
        def _():
            slope_copy(side).wait_recv()
    hidden = slopes[...].astype(jnp.float32) * inner
    field[1, 1 : nx + 1, PAD : PAD + ext, :] = hidden.astype(jnp.bfloat16)
    image = conv(1)
    row = lax.broadcasted_iota(jnp.int32, (1, ext, lanes), 1)
    first = jnp.where(me[2] == 0, PAD, 0)
    last = jnp.where(me[2] == counts[2] - 1, PAD + nz, ext)
    low_image = jnp.where(jnp.logical_and(row >= first, row < last), image, 0.0)
    field[2, 1 : nx + 1, PAD : PAD + ext, :] = low_image.astype(jnp.bfloat16)
    part = image[:, PAD : PAD + nz, :].reshape(nx * nz // 8, 8, lanes)
    squares = jnp.sum(part * part, axis=0)
    start_sum(0, sums_x, sum(squares[:, j : j + 128] for j in range(0, lanes, 128)))
    back = conv(2)
    start_sum(2, sums_z, finish_sum(1, sums_y))
    pulled = slopes[...].astype(jnp.float32) * back
    field[3, 1 : nx + 1, PAD : PAD + ext, :] = pulled.astype(jnp.bfloat16)
    result = conv(3)
    norm = jnp.sqrt(jnp.sum(finish_sum(2, sums_z), keepdims=True) + 1e-06)
    norm_ref[...] = norm
    out_ref[...] = result / norm.reshape(1, 1, 1)

    for r in range(4):
        for i, d in dirs_of(r):
            @pl.when(inside(d, 1))
            def _():
                copy_of(r, i).wait_send()
    for side in range(2):
        @pl.when(inside((0, 0, 2 * side - 1), 1))
        def _():
            slope_copy(side).wait_send()


def on_device(counts, tangent, slopes, first_kernel, second_kernel):
    ch, nx, ny, nz = tangent.shape
    lanes = ny * ch
    full = nz + 4 * PAD
    ext = nz + 2 * PAD

    def spread(array):
        return jnp.transpose(array, (1, 3, 2, 0)).reshape(nx, nz, lanes)

    def flat(array):
        return array.reshape(-1, ch)

    first_t = jnp.swapaxes(first_kernel, 1, 2)
    second_t = jnp.swapaxes(second_kernel, 1, 2)
    most = max(counts)
    result, norm = pl.pallas_call(
        functools.partial(kernel, counts, ch),
        out_shape=(
            jax.ShapeDtypeStruct((nx, nz, lanes), jnp.float32),
            jax.ShapeDtypeStruct((1, 1), jnp.float32),
        ),
        in_specs=[pl.BlockSpec(memory_space=pltpu.VMEM)] * 6,
        out_specs=(pl.BlockSpec(memory_space=pltpu.VMEM),) * 2,
        scratch_shapes=[
            pltpu.VMEM((4, nx + 2, full, lanes), jnp.bfloat16),
            pltpu.VMEM((nx, ext, lanes), jnp.bfloat16),
            pltpu.VMEM((4, 2, full, nx * ch), jnp.bfloat16),
            pltpu.VMEM((4, 2, 2, full * ch // 128, 128), jnp.bfloat16),
            pltpu.VMEM((4, 3, 2, full, nx * ch), jnp.bfloat16),
            pltpu.VMEM((4, 2, 2, full * ch // 128, 128), jnp.bfloat16),
            pltpu.VMEM((2, full, 128), jnp.bfloat16),
            pltpu.VMEM((3, nx + 2, ext, lanes), jnp.bfloat16),
            pltpu.VMEM((nx + 2, ext, lanes), jnp.bfloat16),
            pltpu.VMEM((ext, 4 * lanes), jnp.bfloat16),
            pltpu.VMEM((nx * ext, lanes), jnp.float32),
            pltpu.VMEM((27 * ch, lanes), jnp.float32),
            pltpu.VMEM((2, 12 * lanes, lanes), jnp.bfloat16),
            pltpu.VMEM((counts[0], 8, 128), jnp.float32),
            pltpu.VMEM((counts[1], 8, 128), jnp.float32),
            pltpu.VMEM((counts[2], 8, 128), jnp.float32),
            pltpu.SemaphoreType.DMA((4, len(DIRS))),
            pltpu.SemaphoreType.DMA((4, len(DIRS))),
            pltpu.SemaphoreType.DMA((2,)),
            pltpu.SemaphoreType.DMA((2,)),
            pltpu.SemaphoreType.DMA((3, most)),
            pltpu.SemaphoreType.DMA((3, most)),
        ],
        compiler_params=pltpu.CompilerParams(
            collective_id=0, has_side_effects=True, vmem_limit_bytes=48 * 1024 * 1024
        ),
        name="denoiser_step",
    )(spread(tangent), spread(slopes), flat(first_t), flat(second_t), flat(second_kernel), flat(first_kernel))
    result = result.reshape(nx, nz, ny, ch)
    return (jnp.transpose(result, (3, 0, 2, 1)), norm.reshape(1))


def solution(mesh):
    counts = tuple(mesh.shape[a] for a in AXES)
    return jax.shard_map(
        functools.partial(on_device, counts),
        mesh=mesh,
        in_specs=(P(None, "gx", "gy", "gz"), P(None, "gx", "gy", "gz"), P(), P()),
        out_specs=(P(None, "gx", "gy", "gz"), P()),
        check_vma=False,
    )
```

```python
import functools
import itertools

import jax
import jax.numpy as jnp
from jax import lax
from jax.experimental import pallas as pl
from jax.experimental.pallas import tpu as pltpu
from jax.sharding import PartitionSpec as P

AXES = ("gx", "gy", "gz")
MESH = pl.DeviceIdType.MESH
PAD = 16
DIRS = sorted(
    (d for d in itertools.product((-1, 0, 1), repeat=3) if d != (0, 0, 0)),
    key=lambda d: (d[1:] != (0, 0), sum(map(abs, d)), abs(d[0])),
)


def kernel(
    counts, t_hbm, s_hbm, k1_hbm, k2_hbm, out_ref, norm_ref, t_in, s_in, k1_in, k2_in,
    field, slopes, edge, edge_x, rows, rows_x, line,
    shifted, shifted_y, shifted_x, acc, taps, weights, sums_x, sums_y, sums_z,
    load_sem, send_sem, recv_sem, slope_send, slope_recv, sum_send, sum_recv,
):
    ch, nx, ny, nz = t_in.shape
    lanes = ny * ch
    ext = nz + 2 * PAD
    own = 2 * PAD
    parts = 128 // ch
    per_a = 4 * lanes
    me = tuple(lax.axis_index(a) for a in AXES)

    def inside(d, sign):
        ok = jnp.bool_(True)
        for m, n, s in zip(me, counts, d):
            if s * sign > 0:
                ok = jnp.logical_and(ok, m < n - 1)
            elif s * sign < 0:
                ok = jnp.logical_and(ok, m > 0)
        return ok

    def others(axis):
        n = counts[axis]
        for k in range(1, n):
            there = list(me)
            there[axis] = lax.rem(me[axis] + k, n)
            yield k, tuple(there)

    loads = [
        pltpu.make_async_copy(src, dst, load_sem.at[j])
        for j, (src, dst) in enumerate(
            ((k1_hbm, k1_in), (t_hbm, t_in), (s_hbm, s_in), (k2_hbm, k2_in))
        )
    ]
    for load in loads:
        load.start()

    for buf in (field, slopes, rows, rows_x, line, shifted, shifted_y, shifted_x, weights):
        buf[...] = jnp.zeros_like(buf)

    barrier = pltpu.get_barrier_semaphore()
    total = jnp.int32(0)
    for d in DIRS:
        ok = inside(d, 1)
        total = total + ok.astype(jnp.int32)

        @pl.when(ok)
        def _():
            there = tuple(m + s for m, s in zip(me, d))
            pl.semaphore_signal(barrier, inc=1, device_id=there, device_id_type=MESH)

    for axis in range(3):
        for _, there in others(axis):
            pl.semaphore_signal(barrier, inc=1, device_id=there, device_id_type=MESH)
            total = total + 1

    def remote(src, dst, send, recv, d):
        there = tuple(
            m if s == 0 else jnp.clip(m + s, 0, n - 1) for m, s, n in zip(me, d, counts)
        )
        return pltpu.make_async_remote_copy(
            src_ref=src, dst_ref=dst, send_sem=send, recv_sem=recv,
            device_id=there, device_id_type=MESH,
        )

    def copy_of(r, i):
        dx, dy, dz = DIRS[i]
        if dz == 0:
            z_from, z_to, size = (own, own, nz) if r == 0 else (PAD, PAD, ext)
        elif dz > 0:
            z_from, z_to, size = own + nz - PAD, PAD, PAD
        else:
            z_from, z_to, size = own, own + nz, PAD
        if dy == 0:
            if dx == 0:
                x_from, x_to, planes = 1, 1, nx
            elif dx > 0:
                x_from, x_to, planes = nx, 0, 1
            else:
                x_from, x_to, planes = 1, nx + 1, 1
            src = field.at[r, pl.ds(x_from, planes), pl.ds(z_from, size), :]
            dst = field.at[r, pl.ds(x_to, planes), pl.ds(z_to, size), :]
        elif dx != 0 and dz == 0:
            size = (nz if r == 0 else nz + 4 * PAD) // parts
            src = edge_x.at[r, (dx + 1) // 2, (dy + 1) // 2, pl.ds(0, size), :]
            dst = rows_x.at[r, (dx + 1) // 2, (1 - dy) // 2, pl.ds(0, size), :]
        else:
            src = edge.at[r, (dy + 1) // 2, pl.ds(z_from, size), :]
            dst = rows.at[r, dx + 1, (1 - dy) // 2, pl.ds(z_to, size), :]
        return remote(src, dst, send_sem.at[r, i], recv_sem.at[r, i], DIRS[i])

    def dirs_of(r):
        return [(i, d) for i, d in enumerate(DIRS) if r == 0 or d[2] == 0]

    def slope_copy(side):
        z_from, z_to = (nz, 0) if side else (PAD, nz + PAD)
        return remote(
            slopes.at[:, pl.ds(z_from, PAD), :], slopes.at[:, pl.ds(z_to, PAD), :],
            slope_send.at[side], slope_recv.at[side], (0, 0, 2 * side - 1),
        )

    def sum_copies(axis, buf):
        return [
            pltpu.make_async_remote_copy(
                src_ref=buf.at[me[axis]], dst_ref=buf.at[me[axis]],
                send_sem=sum_send.at[axis, k], recv_sem=sum_recv.at[axis, k],
                device_id=there, device_id_type=MESH,
            )
            for k, there in others(axis)
        ]

    def start_sum(axis, buf, value):
        buf[me[axis]] = value
        for copy in sum_copies(axis, buf):
            copy.start()

    def finish_sum(axis, buf):
        for copy in sum_copies(axis, buf):
            copy.wait()
        result = buf[0]
        for j in range(1, counts[axis]):
            result = result + buf[j]
        return result

    half = 128
    lane_block = lax.broadcasted_iota(jnp.int32, (ch, half), 1) // ch
    lane_inner = lax.rem(lax.broadcasted_iota(jnp.int32, (ch, half), 1), ch)
    tiler = (lax.broadcasted_iota(jnp.int32, (ch, half), 0) == lane_inner)
    tiler = tiler.astype(jnp.float32).astype(jnp.bfloat16)

    def build(r):
        k_in, flip = ((k1_in, 0), (k2_in, 0), (k2_in, 1), (k1_in, 1))[r]
        if flip:
            flat = k_in[...].reshape(27 * ch, ch)
            taps[...] = jnp.dot(flat, tiler, preferred_element_type=jnp.float32)
        else:
            for t in range(27):
                taps[t * ch : (t + 1) * ch, :] = lax.dot_general(
                    k_in[t], tiler, (((0,), (0,)), ((), ())), preferred_element_type=jnp.float32
                )

        def group(g, carry):
            mats = []
            for b in range(3):
                tap = 9 * (g // 3) + 3 * b + g % 3
                tap = 26 - tap if flip else tap
                mats.append(taps[pl.ds(pl.multiple_of(tap * ch, ch), ch), :])

            def strip(y, h):
                tile = jnp.zeros((ch, half), jnp.float32)
                for b in range(3):
                    to = y - (b - 1)
                    if 0 <= to < ny and to // parts == h:
                        tile = jnp.where(lane_block == to % parts, mats[b], tile)
                return tile.astype(jnp.bfloat16)

            base = per_a * (g // 3)
            for h in range(lanes // half):
                y_from, y_to = max(0, h * parts - 1), min(ny, (h + 1) * parts + 1)
                at = pl.multiple_of(base + lanes * (g % 3) + y_from * ch, ch)
                weights[r % 2, pl.ds(at, (y_to - y_from) * ch), h * half : (h + 1) * half] = (
                    jnp.concatenate([strip(y, h) for y in range(y_from, y_to)], axis=0)
                )
            at = pl.multiple_of(base + 3 * lanes + 2 * ch * (g % 3), ch)
            weights[r % 2, pl.ds(at, ch), 0:half] = strip(-1, 0)
            at = pl.multiple_of(at + ch, ch)
            weights[r % 2, pl.ds(at, ch), lanes - half : lanes] = strip(ny, lanes // half - 1)
            return carry

        lax.fori_loop(0, 9, group, 0)

    def spread(ref, x):
        block = jnp.transpose(ref[:, x].astype(jnp.float32), (1, 0, 2))
        return jnp.transpose(block.reshape(lanes, nz), (1, 0)).astype(jnp.bfloat16)

    def conv(r):
        z, size = (own, nz) if r == 0 else (PAD, ext)
        for s in range(2):
            low = s * (ny - 1) * ch
            for x in range(nx):
                edge[r, s, z : z + size, x * ch : (x + 1) * ch] = field[
                    r, 1 + x, z : z + size, low : low + ch
                ]
        start, piece = (own, nz // parts) if r == 0 else (0, (nz + 4 * PAD) // parts)
        for s in range(2):
            low = s * (ny - 1) * ch
            for side, x in enumerate((0, nx - 1)):
                for q in range(parts):
                    z = start + q * piece
                    edge_x[r, side, s, 0:piece, q * ch : (q + 1) * ch] = field[
                        r, 1 + x, z : z + piece, low : low + ch
                    ]
        if r == 0:
            pl.semaphore_wait(barrier, total)
        for i, d in dirs_of(r):
            @pl.when(inside(d, 1))
            def _():
                copy_of(r, i).start()

        def arrive(keep):
            for i, d in dirs_of(r):
                if keep(d):
                    @pl.when(inside(d, -1))
                    def _():
                        copy_of(r, i).wait_recv()

        if r == 0:
            loads[2].wait()
            for x in range(nx):
                slopes[x, PAD : PAD + nz, :] = spread(s_in, x)
            for side in range(2):
                @pl.when(inside((0, 0, 2 * side - 1), 1))
                def _():
                    slope_copy(side).start()

        arrive(lambda d: d[0] == 0 and d[1] == 0)
        lo, size = (PAD, nz) if r == 3 else (0, ext)
        for c in range(3):
            z = PAD - 1 + c + lo
            shifted[c, 1 : nx + 1, lo : lo + size, :] = field[r, 1 : nx + 1, z : z + size, :]

        def weight_rows(first, count):
            return jnp.concatenate(
                [weights[r % 2, a * per_a + first : a * per_a + first + count, :] for a in range(3)],
                axis=0,
            )

        pieces = [
            shifted[c, a : a + nx, lo : lo + size, :].reshape(nx * size, lanes)
            for a in range(3) for c in range(3)
        ]
        acc[0 : nx * size, :] = jnp.dot(
            jnp.concatenate(pieces, axis=1), weight_rows(0, 3 * lanes),
            preferred_element_type=jnp.float32,
        )
        if r == 0:
            loads[3].wait()
        if r < 3:
            build(r + 1)
        arrive(lambda d: d[0] == 0 and d[1] != 0)
        for c in range(3):
            z = PAD - 1 + c + lo
            for s in range(2):
                low = (2 * c + s) * ch
                for x in range(nx):
                    shifted_y[1 + x, lo : lo + size, low : low + ch] = rows[
                        r, 1, s, z : z + size, x * ch : (x + 1) * ch
                    ]
        pieces = [
            shifted_y[a : a + nx, lo : lo + size, :].reshape(nx * size, lanes) for a in range(3)
        ]
        acc[0 : nx * size, :] += jnp.dot(
            jnp.concatenate(pieces, axis=1), weight_rows(3 * lanes, lanes),
            preferred_element_type=jnp.float32,
        )
        if r == 2:
            start_sum(1, sums_y, finish_sum(0, sums_x))
        arrive(lambda d: d[0] != 0)
        for side, plane, out, a in ((1, 0, 0, 0), (0, nx + 1, nx - 1, 2)):
            @pl.when(inside((2 * side - 1, 0, 0), -1))
            def _():
                x = nx - 1 if side else 0
                for s in range(2):
                    if r == 0:
                        for z in (PAD, own + nz):
                            line[s, z : z + PAD, 0:ch] = rows[
                                r, 2 * side, s, z : z + PAD, x * ch : (x + 1) * ch
                            ]
                    for q in range(parts):
                        z = start + q * piece
                        line[s, z : z + piece, 0:ch] = rows_x[
                            r, side, s, 0:piece, q * ch : (q + 1) * ch
                        ]
                for c in range(3):
                    z = PAD - 1 + c + lo
                    shifted_x[lo : lo + size, c * lanes : (c + 1) * lanes] = field[
                        r, plane, z : z + size, :
                    ]
                    for s in range(2):
                        low = 3 * lanes + (2 * c + s) * ch
                        shifted_x[lo : lo + size, low : low + ch] = line[s, z : z + size, 0:ch]
                acc[out * size : (out + 1) * size, :] += jnp.dot(
                    shifted_x[lo : lo + size, :], weights[r % 2, a * per_a : (a + 1) * per_a, :],
                    preferred_element_type=jnp.float32,
                )
        return acc[0 : nx * size, :].reshape(nx, size, lanes)

    loads[0].wait()
    build(0)
    loads[1].wait()
    for x in range(nx):
        field[0, 1 + x, own : own + nz, :] = spread(t_in, x)
    inner = conv(0)
    for side in range(2):
        @pl.when(inside((0, 0, 2 * side - 1), -1))
        def _():
            slope_copy(side).wait_recv()
    hidden = slopes[...].astype(jnp.float32) * inner
    field[1, 1 : nx + 1, PAD : PAD + ext, :] = hidden.astype(jnp.bfloat16)
    image = conv(1)
    row = lax.broadcasted_iota(jnp.int32, (1, ext, lanes), 1)
    first = jnp.where(me[2] == 0, PAD, 0)
    last = jnp.where(me[2] == counts[2] - 1, PAD + nz, ext)
    low_image = jnp.where(jnp.logical_and(row >= first, row < last), image, 0.0)
    field[2, 1 : nx + 1, PAD : PAD + ext, :] = low_image.astype(jnp.bfloat16)
    part = image[:, PAD : PAD + nz, :].reshape(nx * nz // 8, 8, lanes)
    squares = jnp.sum(part * part, axis=0)
    start_sum(0, sums_x, sum(squares[:, j : j + 128] for j in range(0, lanes, 128)))
    back = conv(2)
    start_sum(2, sums_z, finish_sum(1, sums_y))
    pulled = slopes[...].astype(jnp.float32) * back
    field[3, 1 : nx + 1, PAD : PAD + ext, :] = pulled.astype(jnp.bfloat16)
    result = conv(3)
    norm = jnp.sqrt(jnp.sum(finish_sum(2, sums_z), keepdims=True) + 1e-06)
    norm_ref[...] = norm
    out_ref[...] = result / norm.reshape(1, 1, 1)

    for r in range(4):
        for i, d in dirs_of(r):
            @pl.when(inside(d, 1))
            def _():
                copy_of(r, i).wait_send()
    for side in range(2):
        @pl.when(inside((0, 0, 2 * side - 1), 1))
        def _():
            slope_copy(side).wait_send()


def on_device(counts, tangent, slopes, first_kernel, second_kernel):
    ch, nx, ny, nz = tangent.shape
    lanes = ny * ch
    full = nz + 4 * PAD
    ext = nz + 2 * PAD

    most = max(counts)
    result, norm = pl.pallas_call(
        functools.partial(kernel, counts),
        out_shape=(
            jax.ShapeDtypeStruct((nx, nz, lanes), jnp.float32),
            jax.ShapeDtypeStruct((1, 1), jnp.float32),
        ),
        in_specs=[pl.BlockSpec(memory_space=pl.ANY)] * 4,
        out_specs=(pl.BlockSpec(memory_space=pltpu.VMEM),) * 2,
        scratch_shapes=[
            pltpu.VMEM(tangent.shape, jnp.bfloat16),
            pltpu.VMEM(slopes.shape, jnp.bfloat16),
            pltpu.VMEM(first_kernel.shape, jnp.bfloat16),
            pltpu.VMEM(second_kernel.shape, jnp.bfloat16),
            pltpu.VMEM((4, nx + 2, full, lanes), jnp.bfloat16),
            pltpu.VMEM((nx, ext, lanes), jnp.bfloat16),
            pltpu.VMEM((4, 2, full, nx * ch), jnp.bfloat16),
            pltpu.VMEM((4, 2, 2, full * ch // 128, 128), jnp.bfloat16),
            pltpu.VMEM((4, 3, 2, full, nx * ch), jnp.bfloat16),
            pltpu.VMEM((4, 2, 2, full * ch // 128, 128), jnp.bfloat16),
            pltpu.VMEM((2, full, 128), jnp.bfloat16),
            pltpu.VMEM((3, nx + 2, ext, lanes), jnp.bfloat16),
            pltpu.VMEM((nx + 2, ext, lanes), jnp.bfloat16),
            pltpu.VMEM((ext, 4 * lanes), jnp.bfloat16),
            pltpu.VMEM((nx * ext, lanes), jnp.float32),
            pltpu.VMEM((27 * ch, 128), jnp.float32),
            pltpu.VMEM((2, 12 * lanes, lanes), jnp.bfloat16),
            pltpu.VMEM((counts[0], 8, 128), jnp.float32),
            pltpu.VMEM((counts[1], 8, 128), jnp.float32),
            pltpu.VMEM((counts[2], 8, 128), jnp.float32),
            pltpu.SemaphoreType.DMA((4,)),
            pltpu.SemaphoreType.DMA((4, len(DIRS))),
            pltpu.SemaphoreType.DMA((4, len(DIRS))),
            pltpu.SemaphoreType.DMA((2,)),
            pltpu.SemaphoreType.DMA((2,)),
            pltpu.SemaphoreType.DMA((3, most)),
            pltpu.SemaphoreType.DMA((3, most)),
        ],
        compiler_params=pltpu.CompilerParams(
            collective_id=0, has_side_effects=True, vmem_limit_bytes=48 * 1024 * 1024
        ),
        name="denoiser_step",
    )(tangent, slopes, first_kernel, second_kernel)
    result = result.reshape(nx, nz, ny, ch)
    return (jnp.transpose(result, (3, 0, 2, 1)), norm.reshape(1))


def solution(mesh):
    counts = tuple(mesh.shape[a] for a in AXES)
    return jax.shard_map(
        functools.partial(on_device, counts),
        mesh=mesh,
        in_specs=(P(None, "gx", "gy", "gz"), P(None, "gx", "gy", "gz"), P(), P()),
        out_specs=(P(None, "gx", "gy", "gz"), P()),
        check_vma=False,
    )
```

```python
import functools
import itertools

import jax
import jax.numpy as jnp
from jax import lax
from jax.experimental import pallas as pl
from jax.experimental.pallas import tpu as pltpu
from jax.sharding import PartitionSpec as P

AXES = ("gx", "gy", "gz")
MESH = pl.DeviceIdType.MESH
PAD = 16
DIRS = sorted(
    (d for d in itertools.product((-1, 0, 1), repeat=3) if d != (0, 0, 0)),
    key=lambda d: (d[1:] != (0, 0), sum(map(abs, d)), abs(d[0])),
)


def kernel(
    counts, t_hbm, s_hbm, k1_hbm, k2_hbm, out_ref, norm_ref, t_in, s_in, k1_in, k2_in,
    field, slopes, edge, edge_x, rows, rows_x, line,
    shifted, shifted_y, shifted_x, acc, taps, weights, sums_x, sums_y, sums_z,
    load_sem, send_sem, recv_sem, slope_send, slope_recv, sum_send, sum_recv,
):
    ch, nx, ny, nz = t_in.shape
    lanes = ny * ch
    ext = nz + 2 * PAD
    own = 2 * PAD
    parts = 128 // ch
    per_a = 4 * lanes
    me = tuple(lax.axis_index(a) for a in AXES)

    def inside(d, sign):
        ok = jnp.bool_(True)
        for m, n, s in zip(me, counts, d):
            if s * sign > 0:
                ok = jnp.logical_and(ok, m < n - 1)
            elif s * sign < 0:
                ok = jnp.logical_and(ok, m > 0)
        return ok

    def others(axis):
        n = counts[axis]
        for k in range(1, n):
            there = list(me)
            there[axis] = lax.rem(me[axis] + k, n)
            yield k, tuple(there)

    loads = [
        pltpu.make_async_copy(src, dst, load_sem.at[j])
        for j, (src, dst) in enumerate(
            ((k1_hbm, k1_in), (t_hbm, t_in), (s_hbm, s_in), (k2_hbm, k2_in))
        )
    ]
    for load in loads:
        load.start()

    for buf in (field, slopes, rows, rows_x, line, shifted, shifted_y, shifted_x, weights):
        buf[...] = jnp.zeros_like(buf)

    barrier = pltpu.get_barrier_semaphore()
    total = jnp.int32(0)
    for d in DIRS:
        ok = inside(d, 1)
        total = total + ok.astype(jnp.int32)

        @pl.when(ok)
        def _():
            there = tuple(m + s for m, s in zip(me, d))
            pl.semaphore_signal(barrier, inc=1, device_id=there, device_id_type=MESH)

    for axis in range(3):
        for _, there in others(axis):
            pl.semaphore_signal(barrier, inc=1, device_id=there, device_id_type=MESH)
            total = total + 1

    def remote(src, dst, send, recv, d):
        there = tuple(
            m if s == 0 else jnp.clip(m + s, 0, n - 1) for m, s, n in zip(me, d, counts)
        )
        return pltpu.make_async_remote_copy(
            src_ref=src, dst_ref=dst, send_sem=send, recv_sem=recv,
            device_id=there, device_id_type=MESH,
        )

    def copy_of(r, i):
        dx, dy, dz = DIRS[i]
        if dz == 0:
            z_from, z_to, size = (own, own, nz) if r == 0 else (PAD, PAD, ext)
        elif dz > 0:
            z_from, z_to, size = own + nz - PAD, PAD, PAD
        else:
            z_from, z_to, size = own, own + nz, PAD
        if dy == 0:
            if dx == 0:
                x_from, x_to, planes = 1, 1, nx
            elif dx > 0:
                x_from, x_to, planes = nx, 0, 1
            else:
                x_from, x_to, planes = 1, nx + 1, 1
            src = field.at[r, pl.ds(x_from, planes), pl.ds(z_from, size), :]
            dst = field.at[r, pl.ds(x_to, planes), pl.ds(z_to, size), :]
        elif dx != 0 and dz == 0:
            size = (nz if r == 0 else nz + 4 * PAD) // parts
            src = edge_x.at[r, (dx + 1) // 2, (dy + 1) // 2, pl.ds(0, size), :]
            dst = rows_x.at[r, (dx + 1) // 2, (1 - dy) // 2, pl.ds(0, size), :]
        else:
            src = edge.at[r, (dy + 1) // 2, pl.ds(z_from, size), :]
            dst = rows.at[r, dx + 1, (1 - dy) // 2, pl.ds(z_to, size), :]
        return remote(src, dst, send_sem.at[r, i], recv_sem.at[r, i], DIRS[i])

    def dirs_of(r):
        return [(i, d) for i, d in enumerate(DIRS) if r == 0 or d[2] == 0]

    def slope_copy(side):
        z_from, z_to = (nz, 0) if side else (PAD, nz + PAD)
        return remote(
            slopes.at[:, pl.ds(z_from, PAD), :], slopes.at[:, pl.ds(z_to, PAD), :],
            slope_send.at[side], slope_recv.at[side], (0, 0, 2 * side - 1),
        )

    def sum_copies(axis, buf):
        return [
            pltpu.make_async_remote_copy(
                src_ref=buf.at[me[axis]], dst_ref=buf.at[me[axis]],
                send_sem=sum_send.at[axis, k], recv_sem=sum_recv.at[axis, k],
                device_id=there, device_id_type=MESH,
            )
            for k, there in others(axis)
        ]

    def start_sum(axis, buf, value):
        buf[me[axis]] = value
        for copy in sum_copies(axis, buf):
            copy.start()

    def finish_sum(axis, buf):
        for copy in sum_copies(axis, buf):
            copy.wait()
        result = buf[0]
        for j in range(1, counts[axis]):
            result = result + buf[j]
        return result

    half = 128
    lane_block = lax.broadcasted_iota(jnp.int32, (ch, half), 1) // ch
    lane_inner = lax.rem(lax.broadcasted_iota(jnp.int32, (ch, half), 1), ch)
    tiler = (lax.broadcasted_iota(jnp.int32, (ch, half), 0) == lane_inner)
    tiler = tiler.astype(jnp.float32).astype(jnp.bfloat16)

    def build(r):
        k_in, flip = ((k1_in, 0), (k2_in, 0), (k2_in, 1), (k1_in, 1))[r]
        if flip:
            flat = k_in[...].reshape(27 * ch, ch)
            taps[...] = jnp.dot(flat, tiler, preferred_element_type=jnp.float32)
        else:
            for t in range(27):
                taps[t * ch : (t + 1) * ch, :] = lax.dot_general(
                    k_in[t], tiler, (((0,), (0,)), ((), ())), preferred_element_type=jnp.float32
                )

        def group(g, carry):
            mats = []
            for b in range(3):
                tap = 9 * (g // 3) + 3 * b + g % 3
                tap = 26 - tap if flip else tap
                mats.append(taps[pl.ds(pl.multiple_of(tap * ch, ch), ch), :])

            def strip(y, h):
                tile = jnp.zeros((ch, half), jnp.float32)
                for b in range(3):
                    to = y - (b - 1)
                    if 0 <= to < ny and to // parts == h:
                        tile = jnp.where(lane_block == to % parts, mats[b], tile)
                return tile.astype(jnp.bfloat16)

            base = per_a * (g // 3)
            for h in range(lanes // half):
                y_from, y_to = max(0, h * parts - 1), min(ny, (h + 1) * parts + 1)
                at = pl.multiple_of(base + lanes * (g % 3) + y_from * ch, ch)
                weights[r % 2, pl.ds(at, (y_to - y_from) * ch), h * half : (h + 1) * half] = (
                    jnp.concatenate([strip(y, h) for y in range(y_from, y_to)], axis=0)
                )
            at = pl.multiple_of(base + 3 * lanes + 2 * ch * (g % 3), ch)
            weights[r % 2, pl.ds(at, ch), 0:half] = strip(-1, 0)
            at = pl.multiple_of(at + ch, ch)
            weights[r % 2, pl.ds(at, ch), lanes - half : lanes] = strip(ny, lanes // half - 1)
            return carry

        lax.fori_loop(0, 9, group, 0)

    def spread(ref, x):
        block = jnp.transpose(ref[:, x].astype(jnp.float32), (1, 0, 2))
        return jnp.transpose(block.reshape(lanes, nz), (1, 0)).astype(jnp.bfloat16)

    def span(r):
        return (own, nz // parts) if r == 0 else (0, (nz + 4 * PAD) // parts)

    def send(r, keep):
        for i, d in dirs_of(r):
            if keep(d):
                @pl.when(inside(d, 1))
                def _():
                    copy_of(r, i).start()

    def send_face(r, side):
        start, piece = span(r)
        x = nx - 1 if side else 0
        for s in range(2):
            low = s * (ny - 1) * ch
            for q in range(parts):
                z = start + q * piece
                edge_x[r, side, s, 0:piece, q * ch : (q + 1) * ch] = field[
                    r, 1 + x, z : z + piece, low : low + ch
                ]
        send(r, lambda d: d[0] == 2 * side - 1 and d[2] == 0)

    def send_rest(r):
        z, size = (own, nz) if r == 0 else (PAD, ext)
        for s in range(2):
            low = s * (ny - 1) * ch
            for x in range(nx):
                edge[r, s, z : z + size, x * ch : (x + 1) * ch] = field[
                    r, 1 + x, z : z + size, low : low + ch
                ]
        send(r, lambda d: d[0] == 0 or d[2] != 0)

    def emit(r, x):
        if r == 3:
            return
        value = acc[x * ext : (x + 1) * ext, :]
        if r == 1:
            row = lax.broadcasted_iota(jnp.int32, (ext, lanes), 0)
            first = jnp.where(me[2] == 0, PAD, 0)
            last = jnp.where(me[2] == counts[2] - 1, PAD + nz, ext)
            value = jnp.where(jnp.logical_and(row >= first, row < last), value, 0.0)
        else:
            value = slopes[x].astype(jnp.float32) * value
        field[r + 1, 1 + x, PAD : PAD + ext, :] = value.astype(jnp.bfloat16)

    def conv(r):
        start, piece = span(r)

        def arrive(keep):
            for i, d in dirs_of(r):
                if keep(d):
                    @pl.when(inside(d, -1))
                    def _():
                        copy_of(r, i).wait_recv()

        if r == 0:
            loads[2].wait()
            for x in range(nx):
                slopes[x, PAD : PAD + nz, :] = spread(s_in, x)
            for side in range(2):
                @pl.when(inside((0, 0, 2 * side - 1), 1))
                def _():
                    slope_copy(side).start()

        arrive(lambda d: d[0] == 0 and d[1] == 0)
        lo, size = (PAD, nz) if r == 3 else (0, ext)
        for c in range(3):
            z = PAD - 1 + c + lo
            shifted[c, 1 : nx + 1, lo : lo + size, :] = field[r, 1 : nx + 1, z : z + size, :]

        def weight_rows(first, count):
            return jnp.concatenate(
                [weights[r % 2, a * per_a + first : a * per_a + first + count, :] for a in range(3)],
                axis=0,
            )

        pieces = [
            shifted[c, a : a + nx, lo : lo + size, :].reshape(nx * size, lanes)
            for a in range(3) for c in range(3)
        ]
        acc[0 : nx * size, :] = jnp.dot(
            jnp.concatenate(pieces, axis=1), weight_rows(0, 3 * lanes),
            preferred_element_type=jnp.float32,
        )
        if r == 0:
            loads[3].wait()
        if r < 3:
            build(r + 1)
        arrive(lambda d: d[0] == 0 and d[1] != 0)
        for c in range(3):
            z = PAD - 1 + c + lo
            for s in range(2):
                low = (2 * c + s) * ch
                for x in range(nx):
                    shifted_y[1 + x, lo : lo + size, low : low + ch] = rows[
                        r, 1, s, z : z + size, x * ch : (x + 1) * ch
                    ]
        pieces = [
            shifted_y[a : a + nx, lo : lo + size, :].reshape(nx * size, lanes) for a in range(3)
        ]
        acc[0 : nx * size, :] += jnp.dot(
            jnp.concatenate(pieces, axis=1), weight_rows(3 * lanes, lanes),
            preferred_element_type=jnp.float32,
        )
        if r == 0:
            for side in range(2):
                @pl.when(inside((0, 0, 2 * side - 1), -1))
                def _():
                    slope_copy(side).wait_recv()
        if r == 2:
            start_sum(1, sums_y, finish_sum(0, sums_x))
        faces = ((1, 0, 0, 0), (0, nx + 1, nx - 1, 2))
        for x in range(1, nx - 1):
            emit(r, x)
        for side, plane, out, a in faces:
            @pl.when(jnp.logical_not(inside((2 * side - 1, 0, 0), -1)))
            def _():
                emit(r, out)

        arrive(lambda d: d[0] != 0)
        for side, plane, out, a in faces:
            @pl.when(inside((2 * side - 1, 0, 0), -1))
            def _():
                x = nx - 1 if side else 0
                for s in range(2):
                    if r == 0:
                        for z in (PAD, own + nz):
                            line[s, z : z + PAD, 0:ch] = rows[
                                r, 2 * side, s, z : z + PAD, x * ch : (x + 1) * ch
                            ]
                    for q in range(parts):
                        z = start + q * piece
                        line[s, z : z + piece, 0:ch] = rows_x[
                            r, side, s, 0:piece, q * ch : (q + 1) * ch
                        ]
                for c in range(3):
                    z = PAD - 1 + c + lo
                    shifted_x[lo : lo + size, c * lanes : (c + 1) * lanes] = field[
                        r, plane, z : z + size, :
                    ]
                    for s in range(2):
                        low = 3 * lanes + (2 * c + s) * ch
                        shifted_x[lo : lo + size, low : low + ch] = line[s, z : z + size, 0:ch]
                acc[out * size : (out + 1) * size, :] += jnp.dot(
                    shifted_x[lo : lo + size, :], weights[r % 2, a * per_a : (a + 1) * per_a, :],
                    preferred_element_type=jnp.float32,
                )
                emit(r, out)
                if r < 3:
                    send_face(r + 1, 1 - side)

        if r < 3:
            send_rest(r + 1)

    loads[0].wait()
    build(0)
    loads[1].wait()
    for x in range(nx):
        field[0, 1 + x, own : own + nz, :] = spread(t_in, x)
    pl.semaphore_wait(barrier, total)
    for side in range(2):
        send_face(0, side)
    send_rest(0)
    conv(0)
    conv(1)
    squares = jnp.zeros((8, lanes), jnp.float32)
    for x in range(nx):
        part = acc[x * ext + PAD : x * ext + PAD + nz, :].reshape(nz // 8, 8, lanes)
        squares = squares + jnp.sum(part * part, axis=0)
    start_sum(0, sums_x, sum(squares[:, j : j + 128] for j in range(0, lanes, 128)))
    conv(2)
    start_sum(2, sums_z, finish_sum(1, sums_y))
    conv(3)
    norm = jnp.sqrt(jnp.sum(finish_sum(2, sums_z), keepdims=True) + 1e-06)
    norm_ref[...] = norm
    out_ref[...] = (acc[0 : nx * nz, :] / norm).reshape(nx, nz, lanes)

    for r in range(4):
        for i, d in dirs_of(r):
            @pl.when(inside(d, 1))
            def _():
                copy_of(r, i).wait_send()
    for side in range(2):
        @pl.when(inside((0, 0, 2 * side - 1), 1))
        def _():
            slope_copy(side).wait_send()


def on_device(counts, tangent, slopes, first_kernel, second_kernel):
    ch, nx, ny, nz = tangent.shape
    lanes = ny * ch
    full = nz + 4 * PAD
    ext = nz + 2 * PAD

    most = max(counts)
    result, norm = pl.pallas_call(
        functools.partial(kernel, counts),
        out_shape=(
            jax.ShapeDtypeStruct((nx, nz, lanes), jnp.float32),
            jax.ShapeDtypeStruct((1, 1), jnp.float32),
        ),
        in_specs=[pl.BlockSpec(memory_space=pl.ANY)] * 4,
        out_specs=(pl.BlockSpec(memory_space=pltpu.VMEM),) * 2,
        scratch_shapes=[
            pltpu.VMEM(tangent.shape, jnp.bfloat16),
            pltpu.VMEM(slopes.shape, jnp.bfloat16),
            pltpu.VMEM(first_kernel.shape, jnp.bfloat16),
            pltpu.VMEM(second_kernel.shape, jnp.bfloat16),
            pltpu.VMEM((4, nx + 2, full, lanes), jnp.bfloat16),
            pltpu.VMEM((nx, ext, lanes), jnp.bfloat16),
            pltpu.VMEM((4, 2, full, nx * ch), jnp.bfloat16),
            pltpu.VMEM((4, 2, 2, full * ch // 128, 128), jnp.bfloat16),
            pltpu.VMEM((4, 3, 2, full, nx * ch), jnp.bfloat16),
            pltpu.VMEM((4, 2, 2, full * ch // 128, 128), jnp.bfloat16),
            pltpu.VMEM((2, full, 128), jnp.bfloat16),
            pltpu.VMEM((3, nx + 2, ext, lanes), jnp.bfloat16),
            pltpu.VMEM((nx + 2, ext, lanes), jnp.bfloat16),
            pltpu.VMEM((ext, 4 * lanes), jnp.bfloat16),
            pltpu.VMEM((nx * ext, lanes), jnp.float32),
            pltpu.VMEM((27 * ch, 128), jnp.float32),
            pltpu.VMEM((2, 12 * lanes, lanes), jnp.bfloat16),
            pltpu.VMEM((counts[0], 8, 128), jnp.float32),
            pltpu.VMEM((counts[1], 8, 128), jnp.float32),
            pltpu.VMEM((counts[2], 8, 128), jnp.float32),
            pltpu.SemaphoreType.DMA((4,)),
            pltpu.SemaphoreType.DMA((4, len(DIRS))),
            pltpu.SemaphoreType.DMA((4, len(DIRS))),
            pltpu.SemaphoreType.DMA((2,)),
            pltpu.SemaphoreType.DMA((2,)),
            pltpu.SemaphoreType.DMA((3, most)),
            pltpu.SemaphoreType.DMA((3, most)),
        ],
        compiler_params=pltpu.CompilerParams(
            collective_id=0, has_side_effects=True, vmem_limit_bytes=56 * 1024 * 1024
        ),
        name="denoiser_step",
    )(tangent, slopes, first_kernel, second_kernel)
    result = result.reshape(nx, nz, ny, ch)
    return (jnp.transpose(result, (3, 0, 2, 1)), norm.reshape(1))


def solution(mesh):
    counts = tuple(mesh.shape[a] for a in AXES)
    return jax.shard_map(
        functools.partial(on_device, counts),
        mesh=mesh,
        in_specs=(P(None, "gx", "gy", "gz"), P(None, "gx", "gy", "gz"), P(), P()),
        out_specs=(P(None, "gx", "gy", "gz"), P()),
        check_vma=False,
    )
```

```python
import functools
import itertools

import jax
import jax.numpy as jnp
from jax import lax
from jax.experimental import pallas as pl
from jax.experimental.pallas import tpu as pltpu
from jax.sharding import PartitionSpec as P

AXES = ("gx", "gy", "gz")
MESH = pl.DeviceIdType.MESH
PAD = 16
DIRS = sorted(
    (d for d in itertools.product((-1, 0, 1), repeat=3) if d != (0, 0, 0)),
    key=lambda d: (d[1:] != (0, 0), sum(map(abs, d)), abs(d[0])),
)


def kernel(
    counts, t_hbm, s_hbm, k1_hbm, k2_hbm, out_ref, norm_ref, t_in, s_in, k1_in, k2_in,
    field, slopes, edge, edge_x, rows, rows_x, line,
    shifted, shifted_y, shifted_x, acc, taps, weights, sums_x, sums_y, sums_z,
    load_sem, send_sem, recv_sem, slope_send, slope_recv, sum_send, sum_recv,
):
    ch, nx, ny, nz = t_in.shape
    lanes = ny * ch
    ext = nz + 2 * PAD
    own = 2 * PAD
    parts = 128 // ch
    per_a = 4 * lanes
    me = tuple(lax.axis_index(a) for a in AXES)

    def inside(d, sign):
        ok = jnp.bool_(True)
        for m, n, s in zip(me, counts, d):
            if s * sign > 0:
                ok = jnp.logical_and(ok, m < n - 1)
            elif s * sign < 0:
                ok = jnp.logical_and(ok, m > 0)
        return ok

    def others(axis):
        n = counts[axis]
        for k in range(1, n):
            there = list(me)
            there[axis] = lax.rem(me[axis] + k, n)
            yield k, tuple(there)

    loads = [
        pltpu.make_async_copy(src, dst, load_sem.at[j])
        for j, (src, dst) in enumerate(
            ((t_hbm, t_in), (s_hbm, s_in), (k1_hbm, k1_in), (k2_hbm, k2_in))
        )
    ]
    for load in loads:
        load.start()

    def clear(*refs):
        for ref in refs:
            ref[...] = jnp.zeros(ref.shape, ref.dtype)

    clear(rows, rows_x)
    clear(field.at[:, 0], field.at[:, nx + 1])
    for z in (0, own + nz):
        clear(field.at[:, pl.ds(1, nx), pl.ds(z, own), :])
    for z in (0, PAD + nz):
        clear(slopes.at[:, pl.ds(z, PAD), :])

    barrier = pltpu.get_barrier_semaphore()
    total = jnp.int32(0)
    for d in DIRS:
        ok = inside(d, 1)
        total = total + ok.astype(jnp.int32)

        @pl.when(ok)
        def _():
            there = tuple(m + s for m, s in zip(me, d))
            pl.semaphore_signal(barrier, inc=1, device_id=there, device_id_type=MESH)

    for axis in range(3):
        for _, there in others(axis):
            pl.semaphore_signal(barrier, inc=1, device_id=there, device_id_type=MESH)
            total = total + 1

    def remote(src, dst, send, recv, d):
        there = tuple(
            m if s == 0 else jnp.clip(m + s, 0, n - 1) for m, s, n in zip(me, d, counts)
        )
        return pltpu.make_async_remote_copy(
            src_ref=src, dst_ref=dst, send_sem=send, recv_sem=recv,
            device_id=there, device_id_type=MESH,
        )

    def copy_of(r, i):
        dx, dy, dz = DIRS[i]
        if dz == 0:
            z_from, z_to, size = (own, own, nz) if r == 0 else (PAD, PAD, ext)
        elif dz > 0:
            z_from, z_to, size = own + nz - PAD, PAD, PAD
        else:
            z_from, z_to, size = own, own + nz, PAD
        if dy == 0:
            if dx == 0:
                x_from, x_to, planes = 1, 1, nx
            elif dx > 0:
                x_from, x_to, planes = nx, 0, 1
            else:
                x_from, x_to, planes = 1, nx + 1, 1
            src = field.at[r, pl.ds(x_from, planes), pl.ds(z_from, size), :]
            dst = field.at[r, pl.ds(x_to, planes), pl.ds(z_to, size), :]
        elif dx != 0 and dz == 0:
            size = (nz if r == 0 else nz + 4 * PAD) // parts
            src = edge_x.at[r, (dx + 1) // 2, (dy + 1) // 2, pl.ds(0, size), :]
            dst = rows_x.at[r, (dx + 1) // 2, (1 - dy) // 2, pl.ds(0, size), :]
        else:
            src = edge.at[r, (dy + 1) // 2, pl.ds(z_from, size), :]
            dst = rows.at[r, dx + 1, (1 - dy) // 2, pl.ds(z_to, size), :]
        return remote(src, dst, send_sem.at[r, i], recv_sem.at[r, i], DIRS[i])

    def dirs_of(r):
        return [(i, d) for i, d in enumerate(DIRS) if r == 0 or d[2] == 0]

    def slope_copy(side):
        z_from, z_to = (nz, 0) if side else (PAD, nz + PAD)
        return remote(
            slopes.at[:, pl.ds(z_from, PAD), :], slopes.at[:, pl.ds(z_to, PAD), :],
            slope_send.at[side], slope_recv.at[side], (0, 0, 2 * side - 1),
        )

    def sum_copies(axis, buf):
        return [
            pltpu.make_async_remote_copy(
                src_ref=buf.at[me[axis]], dst_ref=buf.at[me[axis]],
                send_sem=sum_send.at[axis, k], recv_sem=sum_recv.at[axis, k],
                device_id=there, device_id_type=MESH,
            )
            for k, there in others(axis)
        ]

    def start_sum(axis, buf, value):
        buf[me[axis]] = value
        for copy in sum_copies(axis, buf):
            copy.start()

    def finish_sum(axis, buf):
        for copy in sum_copies(axis, buf):
            copy.wait()
        result = buf[0]
        for j in range(1, counts[axis]):
            result = result + buf[j]
        return result

    half = 128
    lane_block = lax.broadcasted_iota(jnp.int32, (ch, half), 1) // ch
    lane_inner = lax.rem(lax.broadcasted_iota(jnp.int32, (ch, half), 1), ch)
    tiler = (lax.broadcasted_iota(jnp.int32, (ch, half), 0) == lane_inner)
    tiler = tiler.astype(jnp.float32).astype(jnp.bfloat16)

    def build(r):
        k_in, flip = ((k1_in, 0), (k2_in, 0), (k2_in, 1), (k1_in, 1))[r]
        if flip:
            flat = k_in[...].reshape(27 * ch, ch)
            taps[...] = jnp.dot(flat, tiler, preferred_element_type=jnp.float32)
        else:
            for t in range(27):
                taps[t * ch : (t + 1) * ch, :] = lax.dot_general(
                    k_in[t], tiler, (((0,), (0,)), ((), ())), preferred_element_type=jnp.float32
                )

        def group(g, carry):
            mats = []
            for b in range(3):
                tap = 9 * (g // 3) + 3 * b + g % 3
                tap = 26 - tap if flip else tap
                mats.append(taps[pl.ds(pl.multiple_of(tap * ch, ch), ch), :])

            def strip(y, h):
                tile = jnp.zeros((ch, half), jnp.float32)
                for b in range(3):
                    to = y - (b - 1)
                    if 0 <= to < ny and to // parts == h:
                        tile = jnp.where(lane_block == to % parts, mats[b], tile)
                return tile.astype(jnp.bfloat16)

            base = per_a * (g // 3)
            for h in range(lanes // half):
                y_from, y_to = max(0, h * parts - 1), min(ny, (h + 1) * parts + 1)
                at = pl.multiple_of(base + lanes * (g % 3) + y_from * ch, ch)
                weights[r % 2, pl.ds(at, (y_to - y_from) * ch), h * half : (h + 1) * half] = (
                    jnp.concatenate([strip(y, h) for y in range(y_from, y_to)], axis=0)
                )
            at = pl.multiple_of(base + 3 * lanes + 2 * ch * (g % 3), ch)
            weights[r % 2, pl.ds(at, ch), 0:half] = strip(-1, 0)
            at = pl.multiple_of(at + ch, ch)
            weights[r % 2, pl.ds(at, ch), lanes - half : lanes] = strip(ny, lanes // half - 1)
            return carry

        lax.fori_loop(0, 9, group, 0)

    def spread(ref, x):
        block = jnp.transpose(ref[:, x].astype(jnp.float32), (1, 0, 2))
        return jnp.transpose(block.reshape(lanes, nz), (1, 0)).astype(jnp.bfloat16)

    def span(r):
        return (own, nz // parts) if r == 0 else (0, (nz + 4 * PAD) // parts)

    def send(r, keep):
        for i, d in dirs_of(r):
            if keep(d):
                @pl.when(inside(d, 1))
                def _():
                    copy_of(r, i).start()

    def send_face(r, side):
        start, piece = span(r)
        x = nx - 1 if side else 0
        for s in range(2):
            low = s * (ny - 1) * ch
            for q in range(parts):
                z = start + q * piece
                edge_x[r, side, s, 0:piece, q * ch : (q + 1) * ch] = field[
                    r, 1 + x, z : z + piece, low : low + ch
                ]
        send(r, lambda d: d[0] == 2 * side - 1 and d[2] == 0)

    def send_rest(r):
        z, size = (own, nz) if r == 0 else (PAD, ext)
        for s in range(2):
            low = s * (ny - 1) * ch
            for x in range(nx):
                edge[r, s, z : z + size, x * ch : (x + 1) * ch] = field[
                    r, 1 + x, z : z + size, low : low + ch
                ]
        send(r, lambda d: d[0] == 0 or d[2] != 0)

    def emit(r, x, norm):
        if r == 3:
            block = jnp.transpose(acc[x * nz : (x + 1) * nz, :] / norm, (1, 0))
            out_ref[:, x] = jnp.transpose(block.reshape(ny, ch, nz), (1, 0, 2))
            return
        value = acc[x * ext : (x + 1) * ext, :]
        if r == 1:
            row = lax.broadcasted_iota(jnp.int32, (ext, lanes), 0)
            first = jnp.where(me[2] == 0, PAD, 0)
            last = jnp.where(me[2] == counts[2] - 1, PAD + nz, ext)
            value = jnp.where(jnp.logical_and(row >= first, row < last), value, 0.0)
        else:
            value = slopes[x].astype(jnp.float32) * value
        field[r + 1, 1 + x, PAD : PAD + ext, :] = value.astype(jnp.bfloat16)

    def conv(r):
        start, piece = span(r)

        def arrive(keep):
            for i, d in dirs_of(r):
                if keep(d):
                    @pl.when(inside(d, -1))
                    def _():
                        copy_of(r, i).wait_recv()

        if r == 0:
            loads[1].wait()
            for x in range(nx):
                slopes[x, PAD : PAD + nz, :] = spread(s_in, x)
            for side in range(2):
                @pl.when(inside((0, 0, 2 * side - 1), 1))
                def _():
                    slope_copy(side).start()

        arrive(lambda d: d[0] == 0 and d[1] == 0)
        lo, size = (PAD, nz) if r == 3 else (0, ext)
        for c in range(3):
            z = PAD - 1 + c + lo
            shifted[c, 1 : nx + 1, lo : lo + size, :] = field[r, 1 : nx + 1, z : z + size, :]

        def weight_rows(first, count):
            return jnp.concatenate(
                [weights[r % 2, a * per_a + first : a * per_a + first + count, :] for a in range(3)],
                axis=0,
            )

        pieces = [
            shifted[c, a : a + nx, lo : lo + size, :].reshape(nx * size, lanes)
            for a in range(3) for c in range(3)
        ]
        acc[0 : nx * size, :] = jnp.dot(
            jnp.concatenate(pieces, axis=1), weight_rows(0, 3 * lanes),
            preferred_element_type=jnp.float32,
        )
        if r == 0:
            loads[3].wait()
        if r < 3:
            build(r + 1)
        arrive(lambda d: d[0] == 0 and d[1] != 0)
        for c in range(3):
            z = PAD - 1 + c + lo
            for s in range(2):
                low = (2 * c + s) * ch
                for x in range(nx):
                    shifted_y[1 + x, lo : lo + size, low : low + ch] = rows[
                        r, 1, s, z : z + size, x * ch : (x + 1) * ch
                    ]
        pieces = [
            shifted_y[a : a + nx, lo : lo + size, :].reshape(nx * size, lanes) for a in range(3)
        ]
        acc[0 : nx * size, :] += jnp.dot(
            jnp.concatenate(pieces, axis=1), weight_rows(3 * lanes, lanes),
            preferred_element_type=jnp.float32,
        )
        if r == 0:
            for side in range(2):
                @pl.when(inside((0, 0, 2 * side - 1), -1))
                def _():
                    slope_copy(side).wait_recv()
        if r == 2:
            start_sum(1, sums_y, finish_sum(0, sums_x))
        norm = None
        if r == 3:
            norm = jnp.sqrt(jnp.sum(finish_sum(2, sums_z), keepdims=True) + 1e-06)
            norm_ref[...] = norm
        faces = ((1, 0, 0, 0), (0, nx + 1, nx - 1, 2))
        for x in range(1, nx - 1):
            emit(r, x, norm)
        for side, plane, out, a in faces:
            @pl.when(jnp.logical_not(inside((2 * side - 1, 0, 0), -1)))
            def _():
                emit(r, out, norm)

        arrive(lambda d: d[0] != 0)
        for side, plane, out, a in faces:
            @pl.when(inside((2 * side - 1, 0, 0), -1))
            def _():
                x = nx - 1 if side else 0
                for s in range(2):
                    if r == 0:
                        for z in (PAD, own + nz):
                            line[s, z : z + PAD, 0:ch] = rows[
                                r, 2 * side, s, z : z + PAD, x * ch : (x + 1) * ch
                            ]
                    for q in range(parts):
                        z = start + q * piece
                        line[s, z : z + piece, 0:ch] = rows_x[
                            r, side, s, 0:piece, q * ch : (q + 1) * ch
                        ]
                for c in range(3):
                    z = PAD - 1 + c + lo
                    shifted_x[lo : lo + size, c * lanes : (c + 1) * lanes] = field[
                        r, plane, z : z + size, :
                    ]
                    for s in range(2):
                        low = 3 * lanes + (2 * c + s) * ch
                        shifted_x[lo : lo + size, low : low + ch] = line[s, z : z + size, 0:ch]
                acc[out * size : (out + 1) * size, :] += jnp.dot(
                    shifted_x[lo : lo + size, :], weights[r % 2, a * per_a : (a + 1) * per_a, :],
                    preferred_element_type=jnp.float32,
                )
                emit(r, out, norm)
                if r < 3:
                    send_face(r + 1, 1 - side)

        if r < 3:
            send_rest(r + 1)

    loads[0].wait()
    for x in (0, nx - 1):
        field[0, 1 + x, own : own + nz, :] = spread(t_in, x)
    pl.semaphore_wait(barrier, total)
    for side in range(2):
        send_face(0, side)
    for x in range(1, nx - 1):
        field[0, 1 + x, own : own + nz, :] = spread(t_in, x)
    send_rest(0)
    clear(line, shifted_x, weights, shifted_y)
    clear(shifted.at[:, 0], shifted.at[:, nx + 1])
    loads[2].wait()
    build(0)
    conv(0)
    conv(1)
    squares = jnp.zeros((8, lanes), jnp.float32)
    for x in range(nx):
        part = acc[x * ext + PAD : x * ext + PAD + nz, :].reshape(nz // 8, 8, lanes)
        squares = squares + jnp.sum(part * part, axis=0)
    start_sum(0, sums_x, sum(squares[:, j : j + 128] for j in range(0, lanes, 128)))
    conv(2)
    start_sum(2, sums_z, finish_sum(1, sums_y))
    conv(3)

    for r in range(4):
        for i, d in dirs_of(r):
            @pl.when(inside(d, 1))
            def _():
                copy_of(r, i).wait_send()
    for side in range(2):
        @pl.when(inside((0, 0, 2 * side - 1), 1))
        def _():
            slope_copy(side).wait_send()


def on_device(counts, tangent, slopes, first_kernel, second_kernel):
    ch, nx, ny, nz = tangent.shape
    lanes = ny * ch
    full = nz + 4 * PAD
    ext = nz + 2 * PAD

    most = max(counts)
    result, norm = pl.pallas_call(
        functools.partial(kernel, counts),
        out_shape=(
            jax.ShapeDtypeStruct(tangent.shape, jnp.float32),
            jax.ShapeDtypeStruct((1, 1), jnp.float32),
        ),
        in_specs=[pl.BlockSpec(memory_space=pl.ANY)] * 4,
        out_specs=(pl.BlockSpec(memory_space=pltpu.VMEM),) * 2,
        scratch_shapes=[
            pltpu.VMEM(tangent.shape, jnp.bfloat16),
            pltpu.VMEM(slopes.shape, jnp.bfloat16),
            pltpu.VMEM(first_kernel.shape, jnp.bfloat16),
            pltpu.VMEM(second_kernel.shape, jnp.bfloat16),
            pltpu.VMEM((4, nx + 2, full, lanes), jnp.bfloat16),
            pltpu.VMEM((nx, ext, lanes), jnp.bfloat16),
            pltpu.VMEM((4, 2, full, nx * ch), jnp.bfloat16),
            pltpu.VMEM((4, 2, 2, full * ch // 128, 128), jnp.bfloat16),
            pltpu.VMEM((4, 3, 2, full, nx * ch), jnp.bfloat16),
            pltpu.VMEM((4, 2, 2, full * ch // 128, 128), jnp.bfloat16),
            pltpu.VMEM((2, full, 128), jnp.bfloat16),
            pltpu.VMEM((3, nx + 2, ext, lanes), jnp.bfloat16),
            pltpu.VMEM((nx + 2, ext, lanes), jnp.bfloat16),
            pltpu.VMEM((ext, 4 * lanes), jnp.bfloat16),
            pltpu.VMEM((nx * ext, lanes), jnp.float32),
            pltpu.VMEM((27 * ch, 128), jnp.float32),
            pltpu.VMEM((2, 12 * lanes, lanes), jnp.bfloat16),
            pltpu.VMEM((counts[0], 8, 128), jnp.float32),
            pltpu.VMEM((counts[1], 8, 128), jnp.float32),
            pltpu.VMEM((counts[2], 8, 128), jnp.float32),
            pltpu.SemaphoreType.DMA((4,)),
            pltpu.SemaphoreType.DMA((4, len(DIRS))),
            pltpu.SemaphoreType.DMA((4, len(DIRS))),
            pltpu.SemaphoreType.DMA((2,)),
            pltpu.SemaphoreType.DMA((2,)),
            pltpu.SemaphoreType.DMA((3, most)),
            pltpu.SemaphoreType.DMA((3, most)),
        ],
        compiler_params=pltpu.CompilerParams(
            collective_id=0, has_side_effects=True, vmem_limit_bytes=56 * 1024 * 1024
        ),
        name="denoiser_step",
    )(tangent, slopes, first_kernel, second_kernel)
    return (result, norm.reshape(1))


def solution(mesh):
    counts = tuple(mesh.shape[a] for a in AXES)
    return jax.shard_map(
        functools.partial(on_device, counts),
        mesh=mesh,
        in_specs=(P(None, "gx", "gy", "gz"), P(None, "gx", "gy", "gz"), P(), P()),
        out_specs=(P(None, "gx", "gy", "gz"), P()),
        check_vma=False,
    )
```

```python
import functools
import itertools

import jax
import jax.numpy as jnp
from jax import lax
from jax.experimental import pallas as pl
from jax.experimental.pallas import tpu as pltpu
from jax.sharding import PartitionSpec as P

AXES = ("gx", "gy", "gz")
MESH = pl.DeviceIdType.MESH
PAD = 16
DIRS = sorted(
    (d for d in itertools.product((-1, 0, 1), repeat=3) if d != (0, 0, 0)),
    key=lambda d: (d[1:] != (0, 0), sum(map(abs, d)), abs(d[0])),
)


def kernel(
    counts, t_hbm, s_hbm, k1_hbm, k2_hbm, out_ref, norm_ref, t_in, s_in, k1_in, k2_in,
    field, slopes, edge, edge_x, rows, rows_x, line,
    shifted, shifted_y, shifted_x, acc, taps, weights, sums_x, sums_y, sums_z,
    load_sem, send_sem, recv_sem, slope_send, slope_recv, sum_send, sum_recv,
):
    ch, nx, ny, nz = t_in.shape
    lanes = ny * ch
    ext = nz + 2 * PAD
    own = 2 * PAD
    parts = 128 // ch
    per_a = 4 * lanes
    me = tuple(lax.axis_index(a) for a in AXES)

    def inside(d, sign):
        ok = jnp.bool_(True)
        for m, n, s in zip(me, counts, d):
            if s * sign > 0:
                ok = jnp.logical_and(ok, m < n - 1)
            elif s * sign < 0:
                ok = jnp.logical_and(ok, m > 0)
        return ok

    def others(axis):
        n = counts[axis]
        for k in range(1, n):
            there = list(me)
            there[axis] = lax.rem(me[axis] + k, n)
            yield k, tuple(there)

    loads = [
        pltpu.make_async_copy(src, dst, load_sem.at[j])
        for j, (src, dst) in enumerate(
            ((t_hbm, t_in), (s_hbm, s_in), (k1_hbm, k1_in), (k2_hbm, k2_in))
        )
    ]
    for load in loads:
        load.start()

    def clear(*refs):
        for ref in refs:
            ref[...] = jnp.zeros(ref.shape, ref.dtype)

    clear(rows, rows_x)
    clear(field.at[:, 0], field.at[:, nx + 1])
    for z in (0, own + nz):
        clear(field.at[:, pl.ds(1, nx), pl.ds(z, own), :])
    for z in (0, PAD + nz):
        clear(slopes.at[:, pl.ds(z, PAD), :])

    barrier = pltpu.get_barrier_semaphore()
    total = jnp.int32(0)
    for d in DIRS:
        ok = inside(d, 1)
        total = total + ok.astype(jnp.int32)

        @pl.when(ok)
        def _():
            there = tuple(m + s for m, s in zip(me, d))
            pl.semaphore_signal(barrier, inc=1, device_id=there, device_id_type=MESH)

    for axis in range(3):
        for _, there in others(axis):
            pl.semaphore_signal(barrier, inc=1, device_id=there, device_id_type=MESH)
            total = total + 1

    def remote(src, dst, send, recv, d):
        there = tuple(
            m if s == 0 else jnp.clip(m + s, 0, n - 1) for m, s, n in zip(me, d, counts)
        )
        return pltpu.make_async_remote_copy(
            src_ref=src, dst_ref=dst, send_sem=send, recv_sem=recv,
            device_id=there, device_id_type=MESH,
        )

    def copy_of(r, i):
        dx, dy, dz = DIRS[i]
        if dz == 0:
            z_from, z_to, size = (own, own, nz) if r == 0 else (PAD, PAD, ext)
        elif dz > 0:
            z_from, z_to, size = own + nz - PAD, PAD, PAD
        else:
            z_from, z_to, size = own, own + nz, PAD
        if dy == 0:
            if dx == 0:
                x_from, x_to, planes = 1, 1, nx
            elif dx > 0:
                x_from, x_to, planes = nx, 0, 1
            else:
                x_from, x_to, planes = 1, nx + 1, 1
            src = field.at[r, pl.ds(x_from, planes), pl.ds(z_from, size), :]
            dst = field.at[r, pl.ds(x_to, planes), pl.ds(z_to, size), :]
        elif dx != 0 and dz == 0:
            size = (nz if r == 0 else nz + 4 * PAD) // parts
            src = edge_x.at[r, (dx + 1) // 2, (dy + 1) // 2, pl.ds(0, size), :]
            dst = rows_x.at[r, (dx + 1) // 2, (1 - dy) // 2, pl.ds(0, size), :]
        else:
            src = edge.at[r, (dy + 1) // 2, pl.ds(z_from, size), :]
            dst = rows.at[r, dx + 1, (1 - dy) // 2, pl.ds(z_to, size), :]
        return remote(src, dst, send_sem.at[r, i], recv_sem.at[r, i], DIRS[i])

    def dirs_of(r):
        return [(i, d) for i, d in enumerate(DIRS) if r == 0 or d[2] == 0]

    def slope_copy(side):
        z_from, z_to = (nz, 0) if side else (PAD, nz + PAD)
        return remote(
            slopes.at[:, pl.ds(z_from, PAD), :], slopes.at[:, pl.ds(z_to, PAD), :],
            slope_send.at[side], slope_recv.at[side], (0, 0, 2 * side - 1),
        )

    def sum_copies(axis, buf):
        return [
            pltpu.make_async_remote_copy(
                src_ref=buf.at[me[axis]], dst_ref=buf.at[me[axis]],
                send_sem=sum_send.at[axis, k], recv_sem=sum_recv.at[axis, k],
                device_id=there, device_id_type=MESH,
            )
            for k, there in others(axis)
        ]

    def start_sum(axis, buf, value):
        buf[me[axis]] = value
        for copy in sum_copies(axis, buf):
            copy.start()

    def finish_sum(axis, buf):
        for copy in sum_copies(axis, buf):
            copy.wait()
        result = buf[0]
        for j in range(1, counts[axis]):
            result = result + buf[j]
        return result

    half = 128
    lane_block = lax.broadcasted_iota(jnp.int32, (ch, half), 1) // ch
    lane_inner = lax.rem(lax.broadcasted_iota(jnp.int32, (ch, half), 1), ch)
    tiler = (lax.broadcasted_iota(jnp.int32, (ch, half), 0) == lane_inner)
    tiler = tiler.astype(jnp.float32).astype(jnp.bfloat16)

    def build(r):
        k_in, flip = ((k1_in, 0), (k2_in, 0), (k2_in, 1), (k1_in, 1))[r]
        if flip:
            flat = k_in[...].reshape(27 * ch, ch)
            taps[...] = jnp.dot(flat, tiler, preferred_element_type=jnp.float32)
        else:
            for t in range(27):
                taps[t * ch : (t + 1) * ch, :] = lax.dot_general(
                    k_in[t], tiler, (((0,), (0,)), ((), ())), preferred_element_type=jnp.float32
                )

        def group(g, carry):
            mats = []
            for b in range(3):
                tap = 9 * (g // 3) + 3 * b + g % 3
                tap = 26 - tap if flip else tap
                mats.append(taps[pl.ds(pl.multiple_of(tap * ch, ch), ch), :])

            def strip(y, h):
                tile = jnp.zeros((ch, half), jnp.float32)
                for b in range(3):
                    to = y - (b - 1)
                    if 0 <= to < ny and to // parts == h:
                        tile = jnp.where(lane_block == to % parts, mats[b], tile)
                return tile.astype(jnp.bfloat16)

            base = per_a * (g // 3)
            for h in range(lanes // half):
                y_from, y_to = max(0, h * parts - 1), min(ny, (h + 1) * parts + 1)
                at = pl.multiple_of(base + lanes * (g % 3) + y_from * ch, ch)
                weights[r % 2, pl.ds(at, (y_to - y_from) * ch), h * half : (h + 1) * half] = (
                    jnp.concatenate([strip(y, h) for y in range(y_from, y_to)], axis=0)
                )
            at = pl.multiple_of(base + 3 * lanes + 2 * ch * (g % 3), ch)
            weights[r % 2, pl.ds(at, ch), 0:half] = strip(-1, 0)
            at = pl.multiple_of(at + ch, ch)
            weights[r % 2, pl.ds(at, ch), lanes - half : lanes] = strip(ny, lanes // half - 1)
            return carry

        lax.fori_loop(0, 9, group, 0)

    def spread(ref, x):
        block = jnp.transpose(ref[:, x].astype(jnp.float32), (1, 0, 2))
        return jnp.transpose(block.reshape(lanes, nz), (1, 0)).astype(jnp.bfloat16)

    def span(r):
        return (own, nz // parts) if r == 0 else (0, (nz + 4 * PAD) // parts)

    def send(r, keep):
        for i, d in dirs_of(r):
            if keep(d):
                @pl.when(inside(d, 1))
                def _():
                    copy_of(r, i).start()

    def send_face(r, side):
        start, piece = span(r)
        x = nx - 1 if side else 0
        for s in range(2):
            low = s * (ny - 1) * ch
            for q in range(parts):
                z = start + q * piece
                edge_x[r, side, s, 0:piece, q * ch : (q + 1) * ch] = field[
                    r, 1 + x, z : z + piece, low : low + ch
                ]
        send(r, lambda d: d[0] == 2 * side - 1 and d[2] == 0)

    def send_rest(r):
        z, size = (own, nz) if r == 0 else (PAD, ext)
        for s in range(2):
            low = s * (ny - 1) * ch
            for x in range(nx):
                edge[r, s, z : z + size, x * ch : (x + 1) * ch] = field[
                    r, 1 + x, z : z + size, low : low + ch
                ]
        send(r, lambda d: d[0] == 0 or d[2] != 0)

    def rows_of(r):
        return (PAD, nz) if r == 3 else (PAD // 2, nz + PAD)

    def emit(r, x, norm):
        if r == 3:
            block = jnp.transpose(acc[x * nz : (x + 1) * nz, :] / norm, (1, 0))
            out_ref[:, x] = jnp.transpose(block.reshape(ny, ch, nz), (1, 0, 2))
            return
        lo, size = rows_of(r)
        value = acc[x * size : (x + 1) * size, :]
        if r == 1:
            row = lax.broadcasted_iota(jnp.int32, (size, lanes), 0) + lo
            first = jnp.where(me[2] == 0, PAD, 0)
            last = jnp.where(me[2] == counts[2] - 1, PAD + nz, ext)
            value = jnp.where(jnp.logical_and(row >= first, row < last), value, 0.0)
        else:
            value = slopes[x, lo : lo + size, :].astype(jnp.float32) * value
        field[r + 1, 1 + x, PAD + lo : PAD + lo + size, :] = value.astype(jnp.bfloat16)

    def conv(r):
        start, piece = span(r)

        def arrive(keep):
            for i, d in dirs_of(r):
                if keep(d):
                    @pl.when(inside(d, -1))
                    def _():
                        copy_of(r, i).wait_recv()

        if r == 0:
            loads[1].wait()
            for x in range(nx):
                slopes[x, PAD : PAD + nz, :] = spread(s_in, x)
            for side in range(2):
                @pl.when(inside((0, 0, 2 * side - 1), 1))
                def _():
                    slope_copy(side).start()

        arrive(lambda d: d[0] == 0 and d[1] == 0)
        lo, size = rows_of(r)
        for c in range(3):
            z = PAD - 1 + c + lo
            shifted[1 : nx + 1, 0:size, c * lanes : (c + 1) * lanes] = field[
                r, 1 : nx + 1, z : z + size, :
            ]

        def planes_dot(buf, a, first):
            lhs = buf[a : a + nx, 0:size, :].reshape(nx * size, buf.shape[2])
            base = a * per_a + first
            rhs = weights[r % 2, base : base + buf.shape[2], :]
            return jnp.dot(lhs, rhs, preferred_element_type=jnp.float32)

        acc[0 : nx * size, :] = sum(planes_dot(shifted, a, 0) for a in range(3))
        if r == 0:
            loads[3].wait()
        if r < 3:
            build(r + 1)
        arrive(lambda d: d[0] == 0 and d[1] != 0)
        for c in range(3):
            z = PAD - 1 + c + lo
            for s in range(2):
                low = (2 * c + s) * ch
                for x in range(nx):
                    shifted_y[1 + x, 0:size, low : low + ch] = rows[
                        r, 1, s, z : z + size, x * ch : (x + 1) * ch
                    ]
        acc[0 : nx * size, :] += sum(planes_dot(shifted_y, a, 3 * lanes) for a in range(3))
        if r == 0:
            for side in range(2):
                @pl.when(inside((0, 0, 2 * side - 1), -1))
                def _():
                    slope_copy(side).wait_recv()
        if r == 2:
            start_sum(1, sums_y, finish_sum(0, sums_x))
        norm = None
        if r == 3:
            norm = jnp.sqrt(jnp.sum(finish_sum(2, sums_z), keepdims=True) + 1e-06)
            norm_ref[...] = norm
        faces = ((1, 0, 0, 0), (0, nx + 1, nx - 1, 2))
        for x in range(1, nx - 1):
            emit(r, x, norm)
        for side, plane, out, a in faces:
            @pl.when(jnp.logical_not(inside((2 * side - 1, 0, 0), -1)))
            def _():
                emit(r, out, norm)

        arrive(lambda d: d[0] != 0)
        for side, plane, out, a in faces:
            @pl.when(inside((2 * side - 1, 0, 0), -1))
            def _():
                x = nx - 1 if side else 0
                for s in range(2):
                    if r == 0:
                        for z in (PAD, own + nz):
                            line[s, z : z + PAD, 0:ch] = rows[
                                r, 2 * side, s, z : z + PAD, x * ch : (x + 1) * ch
                            ]
                    for q in range(parts):
                        z = start + q * piece
                        line[s, z : z + piece, 0:ch] = rows_x[
                            r, side, s, 0:piece, q * ch : (q + 1) * ch
                        ]
                for c in range(3):
                    z = PAD - 1 + c + lo
                    shifted_x[0:size, c * lanes : (c + 1) * lanes] = field[
                        r, plane, z : z + size, :
                    ]
                    for s in range(2):
                        low = 3 * lanes + (2 * c + s) * ch
                        shifted_x[0:size, low : low + ch] = line[s, z : z + size, 0:ch]
                acc[out * size : (out + 1) * size, :] += jnp.dot(
                    shifted_x[0:size, :], weights[r % 2, a * per_a : (a + 1) * per_a, :],
                    preferred_element_type=jnp.float32,
                )
                emit(r, out, norm)
                if r < 3:
                    send_face(r + 1, 1 - side)

        if r < 3:
            send_rest(r + 1)

    loads[0].wait()
    for x in (0, nx - 1):
        field[0, 1 + x, own : own + nz, :] = spread(t_in, x)
    pl.semaphore_wait(barrier, total)
    for side in range(2):
        send_face(0, side)
    for x in range(1, nx - 1):
        field[0, 1 + x, own : own + nz, :] = spread(t_in, x)
    send_rest(0)
    clear(line, shifted_x, weights, shifted_y)
    clear(shifted.at[0], shifted.at[nx + 1])
    loads[2].wait()
    build(0)
    conv(0)
    conv(1)
    squares = jnp.zeros((8, lanes), jnp.float32)
    for x in range(nx):
        lo, size = rows_of(1)
        z = x * size + PAD - lo
        part = acc[z : z + nz, :].reshape(nz // 8, 8, lanes)
        squares = squares + jnp.sum(part * part, axis=0)
    start_sum(0, sums_x, sum(squares[:, j : j + 128] for j in range(0, lanes, 128)))
    conv(2)
    start_sum(2, sums_z, finish_sum(1, sums_y))
    conv(3)

    for r in range(4):
        for i, d in dirs_of(r):
            @pl.when(inside(d, 1))
            def _():
                copy_of(r, i).wait_send()
    for side in range(2):
        @pl.when(inside((0, 0, 2 * side - 1), 1))
        def _():
            slope_copy(side).wait_send()


def on_device(counts, tangent, slopes, first_kernel, second_kernel):
    ch, nx, ny, nz = tangent.shape
    lanes = ny * ch
    full = nz + 4 * PAD
    ext = nz + 2 * PAD

    most = max(counts)
    result, norm = pl.pallas_call(
        functools.partial(kernel, counts),
        out_shape=(
            jax.ShapeDtypeStruct(tangent.shape, jnp.float32),
            jax.ShapeDtypeStruct((1, 1), jnp.float32),
        ),
        in_specs=[pl.BlockSpec(memory_space=pl.ANY)] * 4,
        out_specs=(pl.BlockSpec(memory_space=pltpu.VMEM),) * 2,
        scratch_shapes=[
            pltpu.VMEM(tangent.shape, jnp.bfloat16),
            pltpu.VMEM(slopes.shape, jnp.bfloat16),
            pltpu.VMEM(first_kernel.shape, jnp.bfloat16),
            pltpu.VMEM(second_kernel.shape, jnp.bfloat16),
            pltpu.VMEM((4, nx + 2, full, lanes), jnp.bfloat16),
            pltpu.VMEM((nx, ext, lanes), jnp.bfloat16),
            pltpu.VMEM((4, 2, full, nx * ch), jnp.bfloat16),
            pltpu.VMEM((4, 2, 2, full * ch // 128, 128), jnp.bfloat16),
            pltpu.VMEM((4, 3, 2, full, nx * ch), jnp.bfloat16),
            pltpu.VMEM((4, 2, 2, full * ch // 128, 128), jnp.bfloat16),
            pltpu.VMEM((2, full, 128), jnp.bfloat16),
            pltpu.VMEM((nx + 2, ext, 3 * lanes), jnp.bfloat16),
            pltpu.VMEM((nx + 2, ext, lanes), jnp.bfloat16),
            pltpu.VMEM((ext, 4 * lanes), jnp.bfloat16),
            pltpu.VMEM((nx * ext, lanes), jnp.float32),
            pltpu.VMEM((27 * ch, 128), jnp.float32),
            pltpu.VMEM((2, 12 * lanes, lanes), jnp.bfloat16),
            pltpu.VMEM((counts[0], 8, 128), jnp.float32),
            pltpu.VMEM((counts[1], 8, 128), jnp.float32),
            pltpu.VMEM((counts[2], 8, 128), jnp.float32),
            pltpu.SemaphoreType.DMA((4,)),
            pltpu.SemaphoreType.DMA((4, len(DIRS))),
            pltpu.SemaphoreType.DMA((4, len(DIRS))),
            pltpu.SemaphoreType.DMA((2,)),
            pltpu.SemaphoreType.DMA((2,)),
            pltpu.SemaphoreType.DMA((3, most)),
            pltpu.SemaphoreType.DMA((3, most)),
        ],
        compiler_params=pltpu.CompilerParams(
            collective_id=0, has_side_effects=True, vmem_limit_bytes=56 * 1024 * 1024
        ),
        name="denoiser_step",
    )(tangent, slopes, first_kernel, second_kernel)
    return (result, norm.reshape(1))


def solution(mesh):
    counts = tuple(mesh.shape[a] for a in AXES)
    return jax.shard_map(
        functools.partial(on_device, counts),
        mesh=mesh,
        in_specs=(P(None, "gx", "gy", "gz"), P(None, "gx", "gy", "gz"), P(), P()),
        out_specs=(P(None, "gx", "gy", "gz"), P()),
        check_vma=False,
    )
```

```python
import functools
import itertools

import jax
import jax.numpy as jnp
from jax import lax
from jax.experimental import pallas as pl
from jax.experimental.pallas import tpu as pltpu
from jax.sharding import PartitionSpec as P

AXES = ("gx", "gy", "gz")
MESH = pl.DeviceIdType.MESH
PAD = 16
DIRS = sorted(
    (d for d in itertools.product((-1, 0, 1), repeat=3) if d != (0, 0, 0)),
    key=lambda d: (d[1:] != (0, 0), sum(map(abs, d)), abs(d[0])),
)


def kernel(
    counts, t_hbm, s_hbm, k1_hbm, k2_hbm, out_ref, norm_ref, t_in, s_in, k1_in, k2_in,
    field, slopes, edge, edge_x, rows, rows_x, line,
    shifted, shifted_y, shifted_x, acc, taps, weights, sums_x, sums_y, sums_z,
    load_sem, send_sem, recv_sem, slope_send, slope_recv, sum_send, sum_recv,
):
    ch, nx, ny, nz = t_in.shape
    lanes = ny * ch
    ext = nz + 2 * PAD
    own = 2 * PAD
    parts = 128 // ch
    per_a = 4 * lanes
    me = tuple(lax.axis_index(a) for a in AXES)

    def inside(d, sign):
        ok = jnp.bool_(True)
        for m, n, s in zip(me, counts, d):
            if s * sign > 0:
                ok = jnp.logical_and(ok, m < n - 1)
            elif s * sign < 0:
                ok = jnp.logical_and(ok, m > 0)
        return ok

    def others(axis):
        n = counts[axis]
        for k in range(1, n):
            there = list(me)
            there[axis] = lax.rem(me[axis] + k, n)
            yield k, tuple(there)

    loads = [
        pltpu.make_async_copy(src, dst, load_sem.at[j])
        for j, (src, dst) in enumerate(
            ((t_hbm, t_in), (s_hbm, s_in), (k1_hbm, k1_in), (k2_hbm, k2_in))
        )
    ]
    for load in loads:
        load.start()

    def clear(*refs):
        for ref in refs:
            ref[...] = jnp.zeros(ref.shape, ref.dtype)

    clear(rows, rows_x)
    clear(field.at[:, 0], field.at[:, nx + 1])
    for z in (0, own + nz):
        clear(field.at[:, pl.ds(1, nx), pl.ds(z, own), :])
    for z in (0, PAD + nz):
        clear(slopes.at[:, pl.ds(z, PAD), :])

    barrier = pltpu.get_barrier_semaphore()
    total = jnp.int32(0)
    for d in DIRS:
        ok = inside(d, 1)
        total = total + ok.astype(jnp.int32)

        @pl.when(ok)
        def _():
            there = tuple(m + s for m, s in zip(me, d))
            pl.semaphore_signal(barrier, inc=1, device_id=there, device_id_type=MESH)

    for axis in range(3):
        for _, there in others(axis):
            pl.semaphore_signal(barrier, inc=1, device_id=there, device_id_type=MESH)
            total = total + 1

    def remote(src, dst, send, recv, d):
        there = tuple(
            m if s == 0 else jnp.clip(m + s, 0, n - 1) for m, s, n in zip(me, d, counts)
        )
        return pltpu.make_async_remote_copy(
            src_ref=src, dst_ref=dst, send_sem=send, recv_sem=recv,
            device_id=there, device_id_type=MESH,
        )

    def copy_of(r, i):
        dx, dy, dz = DIRS[i]
        if dz == 0:
            z_from, z_to, size = (own, own, nz) if r == 0 else (PAD, PAD, ext)
        elif dz > 0:
            z_from, z_to, size = own + nz - PAD, PAD, PAD
        else:
            z_from, z_to, size = own, own + nz, PAD
        if dy == 0:
            if dx == 0:
                x_from, x_to, planes = 1, 1, nx
            elif dx > 0:
                x_from, x_to, planes = nx, 0, 1
            else:
                x_from, x_to, planes = 1, nx + 1, 1
            src = field.at[r, pl.ds(x_from, planes), pl.ds(z_from, size), :]
            dst = field.at[r, pl.ds(x_to, planes), pl.ds(z_to, size), :]
        elif dx != 0 and dz == 0:
            size = (nz if r == 0 else nz + 4 * PAD) // parts
            src = edge_x.at[r, (dx + 1) // 2, (dy + 1) // 2, pl.ds(0, size), :]
            dst = rows_x.at[r, (dx + 1) // 2, (1 - dy) // 2, pl.ds(0, size), :]
        else:
            src = edge.at[r, (dy + 1) // 2, pl.ds(z_from, size), :]
            dst = rows.at[r, dx + 1, (1 - dy) // 2, pl.ds(z_to, size), :]
        return remote(src, dst, send_sem.at[r, i], recv_sem.at[r, i], DIRS[i])

    def dirs_of(r):
        return [(i, d) for i, d in enumerate(DIRS) if r == 0 or d[2] == 0]

    def slope_copy(side):
        z_from, z_to = (nz, 0) if side else (PAD, nz + PAD)
        return remote(
            slopes.at[:, pl.ds(z_from, PAD), :], slopes.at[:, pl.ds(z_to, PAD), :],
            slope_send.at[side], slope_recv.at[side], (0, 0, 2 * side - 1),
        )

    def sum_copies(axis, buf):
        return [
            pltpu.make_async_remote_copy(
                src_ref=buf.at[me[axis]], dst_ref=buf.at[me[axis]],
                send_sem=sum_send.at[axis, k], recv_sem=sum_recv.at[axis, k],
                device_id=there, device_id_type=MESH,
            )
            for k, there in others(axis)
        ]

    def start_sum(axis, buf, value):
        buf[me[axis]] = value
        for copy in sum_copies(axis, buf):
            copy.start()

    def finish_sum(axis, buf):
        for copy in sum_copies(axis, buf):
            copy.wait()
        result = buf[0]
        for j in range(1, counts[axis]):
            result = result + buf[j]
        return result

    half = 128
    lane_block = lax.broadcasted_iota(jnp.int32, (ch, half), 1) // ch
    lane_inner = lax.rem(lax.broadcasted_iota(jnp.int32, (ch, half), 1), ch)
    tiler = (lax.broadcasted_iota(jnp.int32, (ch, half), 0) == lane_inner)
    tiler = tiler.astype(jnp.float32).astype(jnp.bfloat16)

    def build(r):
        k_in, flip = ((k1_in, 0), (k2_in, 0), (k2_in, 1), (k1_in, 1))[r]
        if flip:
            flat = k_in[...].reshape(27 * ch, ch)
            taps[...] = jnp.dot(flat, tiler, preferred_element_type=jnp.float32)
        else:
            for t in range(27):
                taps[t * ch : (t + 1) * ch, :] = lax.dot_general(
                    k_in[t], tiler, (((0,), (0,)), ((), ())), preferred_element_type=jnp.float32
                )

        def group(g, carry):
            mats = []
            for b in range(3):
                tap = 9 * (g // 3) + 3 * b + g % 3
                tap = 26 - tap if flip else tap
                mats.append(taps[pl.ds(pl.multiple_of(tap * ch, ch), ch), :])

            def strip(y, h):
                tile = jnp.zeros((ch, half), jnp.float32)
                for b in range(3):
                    to = y - (b - 1)
                    if 0 <= to < ny and to // parts == h:
                        tile = jnp.where(lane_block == to % parts, mats[b], tile)
                return tile.astype(jnp.bfloat16)

            base = per_a * (g // 3)
            for h in range(lanes // half):
                y_from, y_to = max(0, h * parts - 1), min(ny, (h + 1) * parts + 1)
                at = pl.multiple_of(base + lanes * (g % 3) + y_from * ch, ch)
                weights[r % 2, pl.ds(at, (y_to - y_from) * ch), h * half : (h + 1) * half] = (
                    jnp.concatenate([strip(y, h) for y in range(y_from, y_to)], axis=0)
                )
            at = pl.multiple_of(base + 3 * lanes + 2 * ch * (g % 3), ch)
            weights[r % 2, pl.ds(at, ch), 0:half] = strip(-1, 0)
            at = pl.multiple_of(at + ch, ch)
            weights[r % 2, pl.ds(at, ch), lanes - half : lanes] = strip(ny, lanes // half - 1)
            return carry

        lax.fori_loop(0, 9, group, 0)

    def spread(ref, x):
        block = jnp.transpose(ref[:, x].astype(jnp.float32), (1, 0, 2))
        return jnp.transpose(block.reshape(lanes, nz), (1, 0)).astype(jnp.bfloat16)

    def span(r):
        return (own, nz // parts) if r == 0 else (0, (nz + 4 * PAD) // parts)

    def send(r, keep):
        for i, d in dirs_of(r):
            if keep(d):
                @pl.when(inside(d, 1))
                def _():
                    copy_of(r, i).start()

    def send_face(r, side):
        start, piece = span(r)
        x = nx - 1 if side else 0
        send(r, lambda d: d == (2 * side - 1, 0, 0))
        for s in range(2):
            low = s * (ny - 1) * ch
            for q in range(parts):
                z = start + q * piece
                edge_x[r, side, s, 0:piece, q * ch : (q + 1) * ch] = field[
                    r, 1 + x, z : z + piece, low : low + ch
                ]
        send(r, lambda d: d[0] == 2 * side - 1 and d[1] != 0 and d[2] == 0)

    def send_rest(r):
        z, size = (own, nz) if r == 0 else (PAD, ext)
        for s in range(2):
            low = s * (ny - 1) * ch
            for x in range(nx):
                edge[r, s, z : z + size, x * ch : (x + 1) * ch] = field[
                    r, 1 + x, z : z + size, low : low + ch
                ]
        send(r, lambda d: d[0] == 0 or d[2] != 0)

    def rows_of(r):
        return (PAD, nz) if r == 3 else (PAD // 2, nz + PAD)

    def emit(r, x, norm):
        if r == 3:
            block = jnp.transpose(acc[x * nz : (x + 1) * nz, :] / norm, (1, 0))
            out_ref[:, x] = jnp.transpose(block.reshape(ny, ch, nz), (1, 0, 2))
            return
        lo, size = rows_of(r)
        value = acc[x * size : (x + 1) * size, :]
        if r == 1:
            row = lax.broadcasted_iota(jnp.int32, (size, lanes), 0) + lo
            first = jnp.where(me[2] == 0, PAD, 0)
            last = jnp.where(me[2] == counts[2] - 1, PAD + nz, ext)
            value = jnp.where(jnp.logical_and(row >= first, row < last), value, 0.0)
        else:
            value = slopes[x, lo : lo + size, :].astype(jnp.float32) * value
        field[r + 1, 1 + x, PAD + lo : PAD + lo + size, :] = value.astype(jnp.bfloat16)

    def conv(r):
        start, piece = span(r)

        def arrive(keep):
            for i, d in dirs_of(r):
                if keep(d):
                    @pl.when(inside(d, -1))
                    def _():
                        copy_of(r, i).wait_recv()

        if r == 0:
            loads[1].wait()
            for x in range(nx):
                slopes[x, PAD : PAD + nz, :] = spread(s_in, x)
            for side in range(2):
                @pl.when(inside((0, 0, 2 * side - 1), 1))
                def _():
                    slope_copy(side).start()

        arrive(lambda d: d[0] == 0 and d[1] == 0)
        lo, size = rows_of(r)
        for c in range(3):
            z = PAD - 1 + c + lo
            shifted[1 : nx + 1, 0:size, c * lanes : (c + 1) * lanes] = field[
                r, 1 : nx + 1, z : z + size, :
            ]

        def planes_dot(buf, a, first):
            lhs = buf[a : a + nx, 0:size, :].reshape(nx * size, buf.shape[2])
            base = a * per_a + first
            rhs = weights[r % 2, base : base + buf.shape[2], :]
            return jnp.dot(lhs, rhs, preferred_element_type=jnp.float32)

        acc[0 : nx * size, :] = sum(planes_dot(shifted, a, 0) for a in range(3))
        if r == 0:
            loads[3].wait()
        if r < 3:
            build(r + 1)
        arrive(lambda d: d[0] == 0 and d[1] != 0)
        for c in range(3):
            z = PAD - 1 + c + lo
            for s in range(2):
                low = (2 * c + s) * ch
                for x in range(nx):
                    shifted_y[1 + x, 0:size, low : low + ch] = rows[
                        r, 1, s, z : z + size, x * ch : (x + 1) * ch
                    ]
        acc[0 : nx * size, :] += sum(planes_dot(shifted_y, a, 3 * lanes) for a in range(3))
        if r == 0:
            for side in range(2):
                @pl.when(inside((0, 0, 2 * side - 1), -1))
                def _():
                    slope_copy(side).wait_recv()
        if r == 2:
            start_sum(1, sums_y, finish_sum(0, sums_x))
        norm = None
        if r == 3:
            norm = jnp.sqrt(jnp.sum(finish_sum(2, sums_z), keepdims=True) + 1e-06)
            norm_ref[...] = norm
        faces = ((1, 0, 0, 0), (0, nx + 1, nx - 1, 2))
        for x in range(1, nx - 1):
            emit(r, x, norm)
        for side, plane, out, a in faces:
            @pl.when(jnp.logical_not(inside((2 * side - 1, 0, 0), -1)))
            def _():
                emit(r, out, norm)

        arrive(lambda d: d[0] != 0 and d[1] == 0)
        for side, plane, out, a in faces:
            @pl.when(inside((2 * side - 1, 0, 0), -1))
            def _():
                x = nx - 1 if side else 0
                base = a * per_a
                for c in range(3):
                    z = PAD - 1 + c + lo
                    shifted_x[0:size, c * lanes : (c + 1) * lanes] = field[
                        r, plane, z : z + size, :
                    ]
                acc[out * size : (out + 1) * size, :] += jnp.dot(
                    shifted_x[0:size, 0 : 3 * lanes],
                    weights[r % 2, base : base + 3 * lanes, :],
                    preferred_element_type=jnp.float32,
                )
                arrive(lambda d: d[0] == 2 * side - 1 and d[1] != 0)
                for s in range(2):
                    if r == 0:
                        for z in (PAD, own + nz):
                            line[s, z : z + PAD, 0:ch] = rows[
                                r, 2 * side, s, z : z + PAD, x * ch : (x + 1) * ch
                            ]
                    for q in range(parts):
                        z = start + q * piece
                        line[s, z : z + piece, 0:ch] = rows_x[
                            r, side, s, 0:piece, q * ch : (q + 1) * ch
                        ]
                for c in range(3):
                    z = PAD - 1 + c + lo
                    for s in range(2):
                        low = 3 * lanes + (2 * c + s) * ch
                        shifted_x[0:size, low : low + ch] = line[s, z : z + size, 0:ch]
                acc[out * size : (out + 1) * size, :] += jnp.dot(
                    shifted_x[0:size, 3 * lanes : per_a],
                    weights[r % 2, base + 3 * lanes : base + per_a, :],
                    preferred_element_type=jnp.float32,
                )
                emit(r, out, norm)
                if r < 3:
                    send_face(r + 1, 1 - side)

        if r < 3:
            send_rest(r + 1)

    loads[0].wait()
    for x in (0, nx - 1):
        field[0, 1 + x, own : own + nz, :] = spread(t_in, x)
    pl.semaphore_wait(barrier, total)
    for side in range(2):
        send_face(0, side)
    for x in range(1, nx - 1):
        field[0, 1 + x, own : own + nz, :] = spread(t_in, x)
    send_rest(0)
    clear(line, shifted_x, weights, shifted_y)
    clear(shifted.at[0], shifted.at[nx + 1])
    loads[2].wait()
    build(0)
    conv(0)
    conv(1)
    squares = jnp.zeros((8, lanes), jnp.float32)
    for x in range(nx):
        lo, size = rows_of(1)
        z = x * size + PAD - lo
        part = acc[z : z + nz, :].reshape(nz // 8, 8, lanes)
        squares = squares + jnp.sum(part * part, axis=0)
    start_sum(0, sums_x, sum(squares[:, j : j + 128] for j in range(0, lanes, 128)))
    conv(2)
    start_sum(2, sums_z, finish_sum(1, sums_y))
    conv(3)

    for r in range(4):
        for i, d in dirs_of(r):
            @pl.when(inside(d, 1))
            def _():
                copy_of(r, i).wait_send()
    for side in range(2):
        @pl.when(inside((0, 0, 2 * side - 1), 1))
        def _():
            slope_copy(side).wait_send()


def on_device(counts, tangent, slopes, first_kernel, second_kernel):
    ch, nx, ny, nz = tangent.shape
    lanes = ny * ch
    full = nz + 4 * PAD
    ext = nz + 2 * PAD

    most = max(counts)
    result, norm = pl.pallas_call(
        functools.partial(kernel, counts),
        out_shape=(
            jax.ShapeDtypeStruct(tangent.shape, jnp.float32),
            jax.ShapeDtypeStruct((1, 1), jnp.float32),
        ),
        in_specs=[pl.BlockSpec(memory_space=pl.ANY)] * 4,
        out_specs=(pl.BlockSpec(memory_space=pltpu.VMEM),) * 2,
        scratch_shapes=[
            pltpu.VMEM(tangent.shape, jnp.bfloat16),
            pltpu.VMEM(slopes.shape, jnp.bfloat16),
            pltpu.VMEM(first_kernel.shape, jnp.bfloat16),
            pltpu.VMEM(second_kernel.shape, jnp.bfloat16),
            pltpu.VMEM((4, nx + 2, full, lanes), jnp.bfloat16),
            pltpu.VMEM((nx, ext, lanes), jnp.bfloat16),
            pltpu.VMEM((4, 2, full, nx * ch), jnp.bfloat16),
            pltpu.VMEM((4, 2, 2, full * ch // 128, 128), jnp.bfloat16),
            pltpu.VMEM((4, 3, 2, full, nx * ch), jnp.bfloat16),
            pltpu.VMEM((4, 2, 2, full * ch // 128, 128), jnp.bfloat16),
            pltpu.VMEM((2, full, 128), jnp.bfloat16),
            pltpu.VMEM((nx + 2, ext, 3 * lanes), jnp.bfloat16),
            pltpu.VMEM((nx + 2, ext, lanes), jnp.bfloat16),
            pltpu.VMEM((ext, 4 * lanes), jnp.bfloat16),
            pltpu.VMEM((nx * ext, lanes), jnp.float32),
            pltpu.VMEM((27 * ch, 128), jnp.float32),
            pltpu.VMEM((2, 12 * lanes, lanes), jnp.bfloat16),
            pltpu.VMEM((counts[0], 8, 128), jnp.float32),
            pltpu.VMEM((counts[1], 8, 128), jnp.float32),
            pltpu.VMEM((counts[2], 8, 128), jnp.float32),
            pltpu.SemaphoreType.DMA((4,)),
            pltpu.SemaphoreType.DMA((4, len(DIRS))),
            pltpu.SemaphoreType.DMA((4, len(DIRS))),
            pltpu.SemaphoreType.DMA((2,)),
            pltpu.SemaphoreType.DMA((2,)),
            pltpu.SemaphoreType.DMA((3, most)),
            pltpu.SemaphoreType.DMA((3, most)),
        ],
        compiler_params=pltpu.CompilerParams(
            collective_id=0, has_side_effects=True, vmem_limit_bytes=56 * 1024 * 1024
        ),
        name="denoiser_step",
    )(tangent, slopes, first_kernel, second_kernel)
    return (result, norm.reshape(1))


def solution(mesh):
    counts = tuple(mesh.shape[a] for a in AXES)
    return jax.shard_map(
        functools.partial(on_device, counts),
        mesh=mesh,
        in_specs=(P(None, "gx", "gy", "gz"), P(None, "gx", "gy", "gz"), P(), P()),
        out_specs=(P(None, "gx", "gy", "gz"), P()),
        check_vma=False,
    )
```
